1024 devices in a mesh: rep: 32 (over x, y, core), blk: 32 (over z).
Axes of the slice: x: 4, y: 4, z: 32, core: 2. Of those that a mesh axis runs over, the one named last changes fastest.
Arguments:
- grad_partial: bfloat16 [32, 512, 32, 512], P('rep', 'blk')
- owner_slot: int32 [32], replicated, may hold values from 0 to 31, each once
- left_root: bfloat16 [32, 512, 512], P('blk', 'rep')
- right_root: bfloat16 [32, 512, 512], P('blk')
- stat_left: float32 [32, 512, 512], P('blk', 'rep'), may hold values from -6 to 6
- stat_right: float32 [32, 512, 512], P('blk', 'rep'), may hold values from -6 to 6
- first_moment: float32 [32, 512, 512], P('blk', 'rep')
- second_moment: float32 [32, 512, 512], P('blk', 'rep'), may hold values from 0.5 to 20
Outputs:
- update: float32 [32, 512, 512], P('blk', 'rep')
- left_next: float32 [32, 512, 512], P('blk', 'rep')
- right_next: float32 [32, 512, 512], P('blk', 'rep')
- moment_one: float32 [32, 512, 512], P('blk', 'rep')
- moment_two: float32 [32, 512, 512], P('blk', 'rep')
The draws below stay inside these ranges and needn't reach their ends.
Inputs may be any that keep to these rules, and one draw needn't show every extreme that they name: `owner_slot`: each slot number appears once.
All inputs are finite; a program needn't handle non-finite values.
Results may differ from the reference program's by a relative error of at most 0.0023.
The reference program's roundings to bfloat16 on the way count: a program that leaves them out, or rounds other values in their place, can miss the bound.
Values may be sent and summed in bfloat16 or wider, within the bound.
A program may use at most 32 MiB of HBM per device.

```python
import math
import jax
import jax.numpy as jnp
from jax import lax

B = 512
NB = 32
N_REP = 32


def draw_grad_partial(key, part):
    key = jax.random.fold_in(key, 11)
    keys = jax.random.split(key, 3)
    rows = jnp.arange(B, dtype=jnp.float32)
    row_scale = jnp.exp(math.log(6.0) * rows / B) * jnp.exp(jax.random.uniform(keys[0], (B,), jnp.float32, 0.0, math.log(3.0)))
    col_scale = jnp.exp(jax.random.uniform(keys[1], (NB, B), jnp.float32, math.log(0.3), math.log(3.0)))
    base = jax.random.normal(keys[2], (N_REP, B, NB, B), jnp.float32)
    scaled = base * row_scale[None, :, None, None] * col_scale[None, None, :, :]
    return (scaled * (1.0 / math.sqrt(N_REP))).astype(jnp.bfloat16)


def root_matrix(key, spread):
    keys = jax.random.split(key, 2)
    diag = jnp.exp(jax.random.uniform(keys[0], (NB, B), jnp.float32, math.log(0.3), math.log(3.0)))
    off = jax.random.normal(keys[1], (NB, B, B), jnp.float32)
    off = (off + jnp.swapaxes(off, 1, 2)) * (spread * 0.7071 / math.sqrt(B))
    return off + jnp.eye(B, dtype=jnp.float32)[None] * diag[:, :, None]


def draw_left_root(key, part):
    key = jax.random.fold_in(key, 23)
    return root_matrix(key, 0.5).astype(jnp.bfloat16)


def draw_right_root(key, part):
    key = jax.random.fold_in(key, 37)
    return root_matrix(key, 0.6).astype(jnp.bfloat16)


def draw_first_moment(key, part):
    key = jax.random.fold_in(key, 53)
    keys = jax.random.split(key, 2)
    rows = jnp.arange(B, dtype=jnp.float32)
    jitter = jnp.exp(jax.random.uniform(keys[0], (NB, B), jnp.float32, 0.0, math.log(2.0)))
    rise = jnp.exp(math.log(9.0) * rows / B)
    base = jax.random.normal(keys[1], (NB, B, B), jnp.float32)
    return base * rise[None, :, None] * jitter[:, :, None]


def level_of(key, dims, shards, low, largest):
    level, own = 1.0, jax.random.fold_in(key, 6)
    for dim, parts in shards:
        steps = jnp.exp(jax.random.uniform(jax.random.fold_in(own, dim), (parts,), jnp.float32, low / len(shards), largest / len(shards)))
        level = level * jnp.repeat(steps, dims[dim] // parts).reshape([-1 if axis == dim else 1 for axis in range(len(dims))])
    return level


def normal_values(rng, extent, deviation, most, cuts=(), kind=jnp.bfloat16):
    loudness = level_of(rng, extent, cuts, -0.22, 0.18) if cuts else 1.0
    entries = jax.random.normal(rng, extent, jnp.float32) * deviation * loudness
    return jnp.minimum(jnp.maximum(entries, -most), most).astype(kind)


def setup_inputs(seed: int = 0) -> dict:
    streams_of = jax.random.split(jax.random.key(seed), 9)
    grad_partial = draw_grad_partial(jax.random.fold_in(streams_of[8], 71), 0)
    owner_slot = jax.random.permutation(streams_of[1], NB).astype(jnp.int32)
    left_root = draw_left_root(jax.random.fold_in(streams_of[8], 71), 0)
    right_root = draw_right_root(jax.random.fold_in(streams_of[8], 71), 0)
    stat_left = normal_values(streams_of[4], (NB, B, B), 1.0, 6.0, ((0, 32), (1, 32)), jnp.float32)
    stat_right = normal_values(streams_of[5], (NB, B, B), 1.0, 6.0, ((0, 32), (1, 32)), jnp.float32)
    first_moment = draw_first_moment(jax.random.fold_in(streams_of[8], 71), 0)
    second_moment = jnp.clip(jnp.exp(math.log(20.0) - 3.6888795 * jax.random.uniform(streams_of[7], (NB, B, B), jnp.float32) ** level_of(streams_of[7], (NB, B, B), ((0, 32), (1, 32)), -0.2, 0.2)), 0.5, 20.0)
    return dict(grad_partial=grad_partial, owner_slot=owner_slot, left_root=left_root, right_root=right_root, stat_left=stat_left, stat_right=stat_right, first_moment=first_moment, second_moment=second_moment)


def reference(grad_partial, owner_slot, left_root, right_root, stat_left, stat_right, first_moment, second_moment):

    def add_replica(total, replica):
        return (total + replica.astype(jnp.float32), None)
    summed, _ = lax.scan(add_replica, jnp.zeros(grad_partial.shape[1:], jnp.float32), grad_partial)
    summed = summed.astype(jnp.bfloat16)
    num_blocks = owner_slot.shape[0]
    block_of = jnp.zeros((num_blocks,), jnp.int32).at[owner_slot].set(jnp.arange(num_blocks, dtype=jnp.int32))

    def one_slot(slot):
        block_id = block_of[slot]
        grad_block = lax.dynamic_index_in_dim(summed, block_id, 1, keepdims=False)
        left = 0.9 * stat_left[slot] + 0.1 * jnp.dot(grad_block, grad_block.T, preferred_element_type=jnp.float32)
        right = 0.9 * stat_right[slot] + 0.1 * jnp.dot(grad_block.T, grad_block, preferred_element_type=jnp.float32)
        half_step = jnp.dot(left_root[slot], grad_block, preferred_element_type=jnp.float32).astype(jnp.bfloat16)
        precond = jnp.dot(half_step, right_root[slot], preferred_element_type=jnp.float32)
        grad_float = grad_block.astype(jnp.float32)
        moment_a = 0.9 * first_moment[slot] + 0.1 * grad_float
        moment_b = 0.95 * second_moment[slot] + 0.05 * grad_float * grad_float
        adam_dir = moment_a / (jnp.sqrt(moment_b) + 1e-08)
        factor = jnp.sqrt(jnp.sum(adam_dir * adam_dir) / (jnp.sum(precond * precond) + 1e-06))
        return (factor * precond, left, right, moment_a, moment_b)
    results = lax.map(one_slot, jnp.arange(num_blocks, dtype=jnp.int32))
    return (results[0], results[1], results[2], results[3], results[4])
```

```python
import jax
import jax.numpy as jnp
from jax import lax
from jax.experimental import pallas as pl
from jax.experimental.pallas import tpu as pltpu
from jax.sharding import PartitionSpec as P

MESH = pl.DeviceIdType.MESH
NX, NY, NC = 4, 4, 2
STEPS = [
    (dx, dy, dc) for dx in range(NX) for dy in range(NY) for dc in range(NC) if dx or dy or dc
]


def step_kernel(
    owner_ref,
    grad_hbm,
    lroot_hbm,
    rroot_hbm,
    sleft_hbm,
    sright_hbm,
    mone_hbm,
    mtwo_hbm,
    update_ref,
    left_ref,
    right_ref,
    one_ref,
    two_ref,
    grad_v,
    ordered,
    land,
    summed,
    gfull,
    lroot_v,
    rroot_v,
    sleft_v,
    sright_v,
    mone_v,
    mtwo_v,
    sums_v,
    sums_land,
    load_sem,
    send_sem,
    recv_sem,
):
    r = lax.axis_index("rep")
    z = lax.axis_index("blk")
    n = NX * NY * NC
    rows = summed.shape[0]
    x, y, c = r // (NY * NC), (r // NC) % NY, r % NC

    def peer_of(step):
        dx, dy, dc = step
        px, py, pc = lax.rem(x + dx, NX), lax.rem(y + dy, NY), lax.rem(c + dc, NC)
        return (px * NY + py) * NC + pc

    loads = [
        pltpu.make_async_copy(src, dst, load_sem.at[k])
        for k, (src, dst) in enumerate(
            [
                (grad_hbm, grad_v),
                (lroot_hbm, lroot_v),
                (rroot_hbm, rroot_v),
                (sleft_hbm, sleft_v),
                (sright_hbm, sright_v),
                (mone_hbm, mone_v),
                (mtwo_hbm, mtwo_v),
            ]
        )
    ]
    loads[0].start()

    barrier = pltpu.get_barrier_semaphore()
    for step in STEPS:
        pl.semaphore_signal(barrier, inc=1, device_id=(peer_of(step), z), device_id_type=MESH)

    @pl.when(r != z)
    def _():
        pl.semaphore_signal(barrier, inc=1, device_id=(z, r), device_id_type=MESH)

    for load in loads[1:]:
        load.start()

    nb = owner_ref.shape[0]
    total_rows = grad_v.shape[0]
    lane = lax.broadcasted_iota(jnp.int32, (1, total_rows), 1)
    target = jnp.zeros((1, total_rows), jnp.int32)
    for b in range(nb):
        target = jnp.where(lane % nb == b, owner_ref[b], target)
    target = target * rows + lane // nb
    loads[0].wait()
    chunk = 128
    for k in range(total_rows // chunk):
        row = lax.broadcasted_iota(jnp.int32, (chunk, total_rows), 0) + k * chunk
        pick = jnp.where(row == target, 1.0, 0.0).astype(jnp.bfloat16)
        part = jnp.dot(pick, grad_v[...], preferred_element_type=jnp.float32)
        ordered[pl.ds(k * chunk, chunk), :] = part.astype(jnp.bfloat16)

    @pl.when(r != z)
    def _():
        pl.semaphore_wait(barrier, n)

    @pl.when(r == z)
    def _():
        pl.semaphore_wait(barrier, n - 1)

    def wait_bytes(ref, sem):
        pltpu.make_async_copy(ref, ref, sem).wait()

    for k, step in enumerate(STEPS):
        peer = peer_of(step)
        pltpu.make_async_remote_copy(
            src_ref=ordered.at[pl.ds(pl.multiple_of(peer * rows, rows), rows), :],
            dst_ref=land.at[pl.ds(k * rows, rows), :],
            send_sem=send_sem.at[0],
            recv_sem=recv_sem.at[0],
            device_id=(peer, z),
            device_id_type=MESH,
        ).start()
    own = pl.ds(pl.multiple_of(r * rows, rows), rows)
    acc = ordered[own, :].astype(jnp.float32)
    wait_bytes(land, recv_sem.at[0])
    for k in range(n - 1):
        acc = acc + land[pl.ds(k * rows, rows), :].astype(jnp.float32)
    slab = acc.astype(jnp.bfloat16)

    @pl.when(r == z)
    def _():
        gfull[own, :] = slab

    @pl.when(r != z)
    def _():
        summed[...] = slab
        across = pltpu.make_async_remote_copy(
            src_ref=summed,
            dst_ref=gfull.at[pl.ds(pl.multiple_of(z * rows, rows), rows), :],
            send_sem=send_sem.at[1],
            recv_sem=recv_sem.at[1],
            device_id=(z, r),
            device_id_type=MESH,
        )
        across.start()
        pltpu.make_async_copy(summed, summed, recv_sem.at[1]).wait()

    for k, step in enumerate(STEPS):
        peer = peer_of(step)
        pltpu.make_async_remote_copy(
            src_ref=gfull.at[own, :],
            dst_ref=gfull.at[own, :],
            send_sem=send_sem.at[2],
            recv_sem=recv_sem.at[2],
            device_id=(peer, z),
            device_id_type=MESH,
        ).start()

    def fold(v):
        v = v * v
        v = sum(v[:, 128 * k : 128 * (k + 1)] for k in range(v.shape[1] // 128))
        return jnp.sum(v, axis=0, keepdims=True)

    for load in loads[1:]:
        load.wait()
    grow = gfull[own, :].astype(jnp.float32)
    one = 0.9 * mone_v[...] + 0.1 * grow
    two = 0.95 * mtwo_v[...] + 0.05 * grow * grow
    one_ref[...] = one
    two_ref[...] = two
    adam = one / (jnp.sqrt(two) + 1e-08)
    adam_part = fold(adam)

    wait_bytes(gfull.at[pl.ds(0, (n - 1) * rows), :], recv_sem.at[2])
    half = jnp.dot(lroot_v[...], gfull[...], preferred_element_type=jnp.float32)
    half = half.astype(jnp.bfloat16)
    precond = jnp.dot(half, rroot_v[...], preferred_element_type=jnp.float32)
    pre_part = fold(precond)
    line = lax.broadcasted_iota(jnp.int32, sums_v.shape, 0)
    sums_v[...] = jnp.where(line == 0, adam_part, jnp.where(line == 1, pre_part, 0.0))
    for k, step in enumerate(STEPS):
        pltpu.make_async_remote_copy(
            src_ref=sums_v,
            dst_ref=sums_land.at[k],
            send_sem=send_sem.at[3],
            recv_sem=recv_sem.at[3],
            device_id=(peer_of(step), z),
            device_id_type=MESH,
        ).start()

    nt = (((1,), (1,)), ((), ()))
    gram = lax.dot_general(gfull[own, :], gfull[...], nt, preferred_element_type=jnp.float32)
    left_ref[...] = 0.9 * sleft_v[...] + 0.1 * gram
    wide = 128
    first = r * rows
    window = pl.ds(pl.multiple_of((first // wide) * wide, wide), wide)
    at = lax.broadcasted_iota(jnp.int32, (rows, wide), 1)
    want = lax.broadcasted_iota(jnp.int32, (rows, wide), 0) + first % wide
    pick = jnp.where(at == want, 1.0, 0.0).astype(jnp.bfloat16)
    cols = lax.dot_general(pick, gfull[:, window], nt, preferred_element_type=jnp.float32)
    gram = jnp.dot(cols.astype(jnp.bfloat16), gfull[...], preferred_element_type=jnp.float32)
    right_ref[...] = 0.9 * sright_v[...] + 0.1 * gram

    wait_bytes(sums_land, recv_sem.at[3])
    sums = sums_v[...]
    for k in range(n - 1):
        sums = sums + sums_land[k]
    adam_sum = jnp.sum(sums[0:1, :], axis=1, keepdims=True)
    pre_sum = jnp.sum(sums[1:2, :], axis=1, keepdims=True)
    update_ref[...] = jnp.sqrt(adam_sum / (pre_sum + 1e-06)) * precond

    wait_bytes(land, send_sem.at[0])

    @pl.when(r != z)
    def _():
        wait_bytes(summed, send_sem.at[1])

    wait_bytes(gfull.at[pl.ds(0, (n - 1) * rows), :], send_sem.at[2])
    wait_bytes(sums_land, send_sem.at[3])


def on_device(
    grad_partial,
    owner_slot,
    left_root,
    right_root,
    stat_left,
    stat_right,
    first_moment,
    second_moment,
):
    _, rows, nb, b = grad_partial.shape
    n = NX * NY * NC
    f32, bf16 = jnp.float32, jnp.bfloat16
    anywhere = pl.BlockSpec(memory_space=pl.ANY)
    vmem = pl.BlockSpec(memory_space=pltpu.VMEM)
    outs = pl.pallas_call(
        step_kernel,
        out_shape=[jax.ShapeDtypeStruct((rows, b), f32)] * 5,
        in_specs=[pl.BlockSpec(memory_space=pltpu.SMEM)] + [anywhere] * 7,
        out_specs=[vmem] * 5,
        scratch_shapes=[
            pltpu.VMEM((rows * nb, b), bf16),
            pltpu.VMEM((rows * nb, b), bf16),
            pltpu.VMEM(((n - 1) * rows, b), bf16),
            pltpu.VMEM((rows, b), bf16),
            pltpu.VMEM((b, b), bf16),
            pltpu.VMEM((rows, b), bf16),
            pltpu.VMEM((b, b), bf16),
            pltpu.VMEM((rows, b), f32),
            pltpu.VMEM((rows, b), f32),
            pltpu.VMEM((rows, b), f32),
            pltpu.VMEM((rows, b), f32),
            pltpu.VMEM((8, 128), f32),
            pltpu.VMEM((n - 1, 8, 128), f32),
            pltpu.SemaphoreType.DMA((7,)),
            pltpu.SemaphoreType.DMA((4,)),
            pltpu.SemaphoreType.DMA((4,)),
        ],
        compiler_params=pltpu.CompilerParams(
            collective_id=0, has_side_effects=True, vmem_limit_bytes=24 * 1024 * 1024
        ),
        name="shampoo_step",
    )(
        owner_slot,
        grad_partial.reshape(rows * nb, b),
        left_root[0],
        right_root[0],
        stat_left[0],
        stat_right[0],
        first_moment[0],
        second_moment[0],
    )
    return tuple(out[None] for out in outs)


def solution(mesh):
    in_specs = (
        P("rep", "blk", None, None),
        P(),
        P("blk", "rep", None),
        P("blk", None, None),
        P("blk", "rep", None),
        P("blk", "rep", None),
        P("blk", "rep", None),
        P("blk", "rep", None),
    )
    out_specs = (P("blk", "rep", None),) * 5
    return jax.shard_map(
        on_device, mesh=mesh, in_specs=in_specs, out_specs=out_specs, check_vma=False
    )
```

```python
import jax
import jax.numpy as jnp
from jax import lax
from jax.experimental import pallas as pl
from jax.experimental.pallas import tpu as pltpu
from jax.sharding import PartitionSpec as P

MESH = pl.DeviceIdType.MESH
NX, NY, NC, NZ = 4, 4, 2, 32
N = NX * NY * NC
NT = (((1,), (1,)), ((), ()))


def chip_distance(step):
    return min(step[0], NX - step[0]) + min(step[1], NY - step[1])


CHIPS = [(dx, dy) for dx in range(NX) for dy in range(NY)]
PEERS = sorted(
    [(dx, dy, dc) for dx, dy in CHIPS for dc in range(NC) if dx or dy or dc],
    key=chip_distance,
    reverse=True,
)


def rep_of(shift):
    high = shift // 16
    rank = high * (2 * (shift - 16)) + (1 - high) * (2 * (15 - shift) + 1)
    tier, k = rank // 8, rank % 8
    core, odd = tier // 2, tier % 2
    j = k + core * (1 - 2 * (k % 2))
    x = j // 2
    y = 2 * (j % 2) + (odd + x) % 2
    return (x * NY + y) * NC + core


def shift_of(rep):
    x, y, core = rep // (NY * NC), (rep // NC) % NY, rep % NC
    j = x * 2 + y // 2
    rank = (2 * core + (x + y) % 2) * 8 + j + core * (1 - 2 * (j % 2))
    odd = rank % 2
    return (1 - odd) * (16 + rank // 2) + odd * (15 - rank // 2)


def step_kernel(
    owner_hbm,
    grad_hbm,
    lroot_hbm,
    rroot_hbm,
    sleft_hbm,
    sright_hbm,
    mone_hbm,
    mtwo_hbm,
    update_ref,
    left_ref,
    right_ref,
    one_ref,
    two_ref,
    owner_s,
    grad_v,
    ordered,
    land,
    summed,
    gfull,
    lfull,
    rroot_v,
    sleft_v,
    sright_v,
    moments_v,
    moments_land,
    pre_v,
    sums_v,
    sums_land,
    load_sem,
    send_sem,
    recv_sem,
    plane_sem,
    far_sem,
):
    r = lax.axis_index("rep")
    z = lax.axis_index("blk")
    rows = summed.shape[0]
    x, y, c = r // (NY * NC), (r // NC) % NY, r % NC
    shift = shift_of(r)
    up = (z + shift) % NZ
    down = (z + NZ - shift) % NZ
    sibling = r + 1 - 2 * c

    def peer_of(step):
        dx, dy, dc = step
        return (((x + dx) % NX) * NY + (y + dy) % NY) * NC + (c + dc) % NC

    def slab_of(index):
        return pl.ds(pl.multiple_of(index * rows, rows), rows)

    def remote(src, dst, k, rep, blk):
        return pltpu.make_async_remote_copy(
            src_ref=src,
            dst_ref=dst,
            send_sem=send_sem.at[k],
            recv_sem=recv_sem.at[k],
            device_id=(rep, blk),
            device_id_type=MESH,
        )

    def wait_bytes(ref, sem):
        pltpu.make_async_copy(ref, ref, sem).wait()

    own = slab_of(r)
    pairs = [
        (grad_hbm, grad_v),
        (owner_hbm, owner_s),
        (lroot_hbm, lfull.at[own, :]),
        (mone_hbm, moments_v.at[0]),
        (mtwo_hbm, moments_v.at[1]),
        (rroot_hbm, rroot_v),
        (sleft_hbm, sleft_v),
        (sright_hbm, sright_v),
    ]
    loads = [pltpu.make_async_copy(src, dst, load_sem.at[k]) for k, (src, dst) in enumerate(pairs)]
    loads[0].start()
    loads[1].start()

    barrier = pltpu.get_barrier_semaphore()
    for dx, dy in CHIPS:
        chip = peer_of((dx, dy, 0)) - c

        @pl.when(chip != r)
        def _():
            pl.semaphore_signal(barrier, inc=1, device_id=(chip, z), device_id_type=MESH)

    @pl.when(shift != 0)
    def _():
        pl.semaphore_signal(barrier, inc=1, device_id=(r - c + 1, down), device_id_type=MESH)

    for load in loads[2:]:
        load.start()

    total_rows = grad_v.shape[0]
    nb = total_rows // rows
    lane = lax.broadcasted_iota(jnp.int32, (1, total_rows), 1)
    loads[1].wait()
    target = jnp.zeros((1, total_rows), jnp.int32)
    for b in range(nb):
        target = jnp.where(lane % nb == b, owner_s[b], target)
    target = rep_of((target + (NZ - z)) % NZ) * rows + lane // nb
    loads[0].wait()
    chunk = 128
    for k in range(total_rows // chunk):
        row = lax.broadcasted_iota(jnp.int32, (chunk, total_rows), 0) + k * chunk
        pick = jnp.where(row == target, 1.0, 0.0).astype(jnp.bfloat16)
        part = jnp.dot(pick, grad_v[...], preferred_element_type=jnp.float32)
        ordered[pl.ds(k * chunk, chunk), :] = part.astype(jnp.bfloat16)

    @pl.when(c == 0)
    def _():
        pl.semaphore_wait(barrier, N - 1)
        pl.semaphore_signal(plane_sem, inc=1, device_id=(sibling, z), device_id_type=MESH)

    @pl.when(c == 1)
    def _():
        pl.semaphore_wait(plane_sem, 1)

    for tier in range(4):
        core, odd = tier // 2, tier % 2
        for dx in (2, 1, 3, 0):
            for m in (1, 0):
                px = (x + dx) % NX
                py = (y + 2 * m + (odd + px + y) % 2) % NY
                peer = (px * NY + py) * NC + core

                @pl.when(peer != r)
                def _():
                    remote(ordered.at[slab_of(peer), :], land.at[own, :], 0, peer, z).start()

    land[own, :] = ordered[own, :]

    @pl.when(c == 1)
    def _():
        mate = shift_of(sibling)

        @pl.when((shift != 0) & (mate != 0))
        def _():
            pl.semaphore_wait(barrier, 2)

        @pl.when((shift == 0) | (mate == 0))
        def _():
            pl.semaphore_wait(barrier, 1)

        pl.semaphore_signal(far_sem, inc=1, device_id=(sibling, z), device_id_type=MESH)

    @pl.when(c == 0)
    def _():
        pl.semaphore_wait(far_sem, 1)

    wait_bytes(land.at[pl.ds(0, (N - 1) * rows), :], recv_sem.at[0])
    acc = land[pl.ds(0, rows), :].astype(jnp.float32)
    for k in range(1, N):
        acc = acc + land[pl.ds(k * rows, rows), :].astype(jnp.float32)
    slab = acc.astype(jnp.bfloat16)
    came = slab_of(down)

    @pl.when(shift == 0)
    def _():
        gfull[came, :] = slab

    @pl.when(shift != 0)
    def _():
        summed[...] = slab
        remote(summed, gfull.at[slab_of(z), :], 1, r, up).start()

    loads[2].wait()
    for step in PEERS:
        remote(lfull.at[own, :], lfull.at[own, :], 2, peer_of(step), z).start()
    loads[3].wait()
    loads[4].wait()
    holder = rep_of((z + NZ - r) % NZ)

    @pl.when(holder == r)
    def _():
        moments_land[...] = moments_v[...]

    @pl.when(holder != r)
    def _():
        remote(moments_v, moments_land, 3, holder, z).start()
        wait_bytes(moments_v, recv_sem.at[3])

    @pl.when(shift != 0)
    def _():
        wait_bytes(summed, recv_sem.at[1])

    for step in PEERS:
        remote(gfull.at[came, :], gfull.at[came, :], 4, peer_of(step), z).start()

    def blend(moments, grad):
        one = 0.9 * moments[0] + 0.1 * grad
        two = 0.95 * moments[1] + 0.05 * grad * grad
        return one, two

    def fold(v):
        v = v * v
        v = sum(v[:, 128 * k : 128 * (k + 1)] for k in range(v.shape[1] // 128))
        return jnp.sum(v, axis=0, keepdims=True)

    one, two = blend(moments_land[...], gfull[came, :].astype(jnp.float32))
    adam_part = fold(one / (jnp.sqrt(two) + 1e-08))
    sums_v[...] = adam_part
    sums_land[r] = adam_part
    for step in PEERS:
        remote(sums_v, sums_land.at[r], 5, peer_of(step), z).start()

    for load in loads[5:]:
        load.wait()
    wait_bytes(lfull.at[pl.ds(0, (N - 1) * rows), :], recv_sem.at[2])
    wait_bytes(gfull.at[pl.ds(0, (N - 1) * rows), :], recv_sem.at[4])
    pre_part = jnp.zeros((1, 128), jnp.float32)
    for k in range(total_rows // chunk):
        part = pl.ds(k * chunk, chunk)
        half = jnp.dot(lfull[part, :], gfull[...], preferred_element_type=jnp.float32)
        precond = jnp.dot(
            half.astype(jnp.bfloat16), rroot_v[...], preferred_element_type=jnp.float32
        )
        pre_v[part, :] = precond
        pre_part = pre_part + fold(precond)

    gram = lax.dot_general(gfull[own, :], gfull[...], NT, preferred_element_type=jnp.float32)
    left_ref[...] = 0.9 * sleft_v[...] + 0.1 * gram
    wide = 128
    first = r * rows
    window = pl.ds(pl.multiple_of((first // wide) * wide, wide), wide)
    at = lax.broadcasted_iota(jnp.int32, (rows, wide), 1)
    want = lax.broadcasted_iota(jnp.int32, (rows, wide), 0) + first % wide
    pick = jnp.where(at == want, 1.0, 0.0).astype(jnp.bfloat16)
    cols = lax.dot_general(pick, gfull[:, window], NT, preferred_element_type=jnp.float32)
    gram = jnp.dot(cols.astype(jnp.bfloat16), gfull[...], preferred_element_type=jnp.float32)
    right_ref[...] = 0.9 * sright_v[...] + 0.1 * gram
    one, two = blend(moments_v[...], gfull[own, :].astype(jnp.float32))
    one_ref[...] = one
    two_ref[...] = two

    wait_bytes(sums_land.at[pl.ds(0, N - 1)], recv_sem.at[5])
    adam_sum = jnp.sum(jnp.sum(sums_land[...], axis=0), axis=1, keepdims=True)
    pre_sum = jnp.sum(pre_part, axis=1, keepdims=True)
    update_ref[...] = jnp.sqrt(adam_sum / (pre_sum + 1e-06)) * pre_v[own, :]

    wait_bytes(land.at[pl.ds(0, (N - 1) * rows), :], send_sem.at[0])

    @pl.when(shift != 0)
    def _():
        wait_bytes(summed, send_sem.at[1])

    wait_bytes(lfull.at[pl.ds(0, (N - 1) * rows), :], send_sem.at[2])

    @pl.when(holder != r)
    def _():
        wait_bytes(moments_v, send_sem.at[3])

    wait_bytes(gfull.at[pl.ds(0, (N - 1) * rows), :], send_sem.at[4])
    wait_bytes(sums_land.at[pl.ds(0, N - 1)], send_sem.at[5])


def store_kernel(*refs):
    half = len(refs) // 2
    for src, dst in zip(refs[:half], refs[half:]):
        dst[...] = src[...]


def on_device(
    grad_partial,
    owner_slot,
    left_root,
    right_root,
    stat_left,
    stat_right,
    first_moment,
    second_moment,
):
    _, rows, nb, b = grad_partial.shape
    f32, bf16 = jnp.float32, jnp.bfloat16
    hbm = pl.BlockSpec(memory_space=pltpu.HBM)
    vmem = pl.BlockSpec(memory_space=pltpu.VMEM)
    shapes = [jax.ShapeDtypeStruct((rows, b), f32)] * 5
    outs = pl.pallas_call(
        step_kernel,
        out_shape=shapes,
        in_specs=[hbm] * 8,
        out_specs=[vmem] * 5,
        scratch_shapes=[
            pltpu.SMEM((nb,), jnp.int32),
            pltpu.VMEM((rows * nb, b), bf16),
            pltpu.VMEM((rows * nb, b), bf16),
            pltpu.VMEM((rows * N, b), bf16),
            pltpu.VMEM((rows, b), bf16),
            pltpu.VMEM((b, b), bf16),
            pltpu.VMEM((b, b), bf16),
            pltpu.VMEM((b, b), bf16),
            pltpu.VMEM((rows, b), f32),
            pltpu.VMEM((rows, b), f32),
            pltpu.VMEM((2, rows, b), f32),
            pltpu.VMEM((2, rows, b), f32),
            pltpu.VMEM((b, b), f32),
            pltpu.VMEM((1, 128), f32),
            pltpu.VMEM((N, 1, 128), f32),
            pltpu.SemaphoreType.DMA((8,)),
            pltpu.SemaphoreType.DMA((6,)),
            pltpu.SemaphoreType.DMA((6,)),
            pltpu.SemaphoreType.REGULAR,
            pltpu.SemaphoreType.REGULAR,
        ],
        compiler_params=pltpu.CompilerParams(
            collective_id=0, has_side_effects=True, vmem_limit_bytes=32 * 1024 * 1024
        ),
        name="shampoo_step",
    )(
        *[
            pltpu.with_memory_space_constraint(v, pltpu.HBM)
            for v in (
                owner_slot,
                grad_partial.reshape(rows * nb, b),
                left_root[0],
                right_root[0],
                stat_left[0],
                stat_right[0],
                first_moment[0],
                second_moment[0],
            )
        ]
    )
    outs = pl.pallas_call(
        store_kernel,
        out_shape=shapes,
        in_specs=[vmem] * 5,
        out_specs=[vmem] * 5,
        compiler_params=pltpu.CompilerParams(vmem_limit_bytes=4 * 1024 * 1024),
        name="store_results",
    )(*outs)
    return tuple(out[None] for out in outs)


def solution(mesh):
    in_specs = (
        P("rep", "blk", None, None),
        P(),
        P("blk", "rep", None),
        P("blk", None, None),
        P("blk", "rep", None),
        P("blk", "rep", None),
        P("blk", "rep", None),
        P("blk", "rep", None),
    )
    out_specs = (P("blk", "rep", None),) * 5
    return jax.shard_map(
        on_device, mesh=mesh, in_specs=in_specs, out_specs=out_specs, check_vma=False
    )
```

```python
import jax
import jax.numpy as jnp
from jax import lax
from jax.experimental import pallas as pl
from jax.experimental.pallas import tpu as pltpu
from jax.sharding import PartitionSpec as P

MESH = pl.DeviceIdType.MESH
NX, NY, NC, NZ = 4, 4, 2, 32
N = NX * NY * NC
NT = (((1,), (1,)), ((), ()))


def chip_distance(step):
    return min(step[0], NX - step[0]) + min(step[1], NY - step[1])


CHIPS = [(dx, dy) for dx in range(NX) for dy in range(NY)]
PEERS = sorted(
    [(dx, dy, dc) for dx, dy in CHIPS for dc in range(NC) if dx or dy or dc],
    key=chip_distance,
    reverse=True,
)


FAR = (0, 1, 2, 7, 4, 5, 6, 3)
NEAR = (1, 0, 3, 2, 5, 4, 7, 6)


def entry(table, k):
    value = table[0] + 0 * k
    for i in range(1, len(table)):
        value = jnp.where(k == i, table[i], value)
    return value


def rep_of(shift):
    high = shift // 16
    rank = high * (2 * (shift - 16)) + (1 - high) * (2 * (15 - shift) + 1)
    tier, k = rank // 8, rank % 8
    core, odd = tier // 2, tier % 2
    j = (1 - core) * entry(FAR, k) + core * entry(NEAR, k)
    x = j // 2
    y = 2 * (j % 2) + (odd + x) % 2
    return (x * NY + y) * NC + core


def shift_of(rep):
    x, y, core = rep // (NY * NC), (rep // NC) % NY, rep % NC
    j = x * 2 + y // 2
    far = entry([FAR.index(i) for i in range(8)], j)
    near = entry([NEAR.index(i) for i in range(8)], j)
    rank = (2 * core + (x + y) % 2) * 8 + (1 - core) * far + core * near
    odd = rank % 2
    return (1 - odd) * (16 + rank // 2) + odd * (15 - rank // 2)


def step_kernel(
    owner_hbm,
    grad_hbm,
    lroot_hbm,
    rroot_hbm,
    sleft_hbm,
    sright_hbm,
    mone_hbm,
    mtwo_hbm,
    update_ref,
    left_ref,
    right_ref,
    one_ref,
    two_ref,
    owner_s,
    grad_v,
    ordered,
    land,
    summed,
    gfull,
    lfull,
    rroot_v,
    sleft_v,
    sright_v,
    moments_v,
    moments_land,
    half_v,
    pre_v,
    sums_v,
    sums_land,
    load_sem,
    send_sem,
    recv_sem,
    slab_sem,
    plane_sem,
    far_sem,
):
    r = lax.axis_index("rep")
    z = lax.axis_index("blk")
    rows = summed.shape[0]
    x, y, c = r // (NY * NC), (r // NC) % NY, r % NC
    shift = shift_of(r)
    up = (z + shift) % NZ
    down = (z + NZ - shift) % NZ
    sibling = r + 1 - 2 * c

    def peer_of(step):
        dx, dy, dc = step
        return (((x + dx) % NX) * NY + (y + dy) % NY) * NC + (c + dc) % NC

    def slab_of(index):
        return pl.ds(pl.multiple_of(index * rows, rows), rows)

    def remote(src, dst, k, rep, blk):
        return pltpu.make_async_remote_copy(
            src_ref=src,
            dst_ref=dst,
            send_sem=send_sem.at[k],
            recv_sem=recv_sem.at[k],
            device_id=(rep, blk),
            device_id_type=MESH,
        )

    def wait_bytes(ref, sem):
        pltpu.make_async_copy(ref, ref, sem).wait()

    own = slab_of(r)
    pairs = [
        (grad_hbm, grad_v),
        (owner_hbm, owner_s),
        (lroot_hbm, lfull.at[own, :]),
        (mone_hbm, moments_v.at[0]),
        (mtwo_hbm, moments_v.at[1]),
        (rroot_hbm, rroot_v),
        (sleft_hbm, sleft_v),
        (sright_hbm, sright_v),
    ]
    loads = [pltpu.make_async_copy(src, dst, load_sem.at[k]) for k, (src, dst) in enumerate(pairs)]
    loads[0].start()
    loads[1].start()

    barrier = pltpu.get_barrier_semaphore()
    for dx, dy in sorted(CHIPS, key=chip_distance, reverse=True):
        chip = peer_of((dx, dy, 0)) - c

        @pl.when(chip != r)
        def _():
            pl.semaphore_signal(barrier, inc=1, device_id=(chip, z), device_id_type=MESH)

    @pl.when(shift != 0)
    def _():
        pl.semaphore_signal(barrier, inc=1, device_id=(r - c + 1, down), device_id_type=MESH)

    for load in loads[2:]:
        load.start()

    total_rows = grad_v.shape[0]
    nb = total_rows // rows
    lane = lax.broadcasted_iota(jnp.int32, (1, total_rows), 1)
    loads[1].wait()
    target = jnp.zeros((1, total_rows), jnp.int32)
    for b in range(nb):
        target = jnp.where(lane % nb == b, owner_s[b], target)
    target = rep_of((target + (NZ - z)) % NZ) * rows + lane // nb
    loads[0].wait()
    chunk = 128
    for k in range(total_rows // chunk):
        row = lax.broadcasted_iota(jnp.int32, (chunk, total_rows), 0) + k * chunk
        pick = jnp.where(row == target, 1.0, 0.0).astype(jnp.bfloat16)
        part = jnp.dot(pick, grad_v[...], preferred_element_type=jnp.float32)
        ordered[pl.ds(k * chunk, chunk), :] = part.astype(jnp.bfloat16)

    @pl.when(c == 0)
    def _():
        pl.semaphore_wait(barrier, N - 1)
        pl.semaphore_signal(plane_sem, inc=1, device_id=(sibling, z), device_id_type=MESH)

    @pl.when(c == 1)
    def _():
        pl.semaphore_wait(plane_sem, 1)

    for tier in range(4):
        core, odd = tier // 2, tier % 2
        for dx, m in ((2, 1), (2, 0), (1, 1), (3, 1), (0, 1), (1, 0), (3, 0), (0, 0)):
            px = (x + dx) % NX
            py = (y + 2 * m + (odd + px + y) % 2) % NY
            peer = (px * NY + py) * NC + core

            @pl.when(peer != r)
            def _():
                remote(ordered.at[slab_of(peer), :], land.at[own, :], 0, peer, z).start()

    land[own, :] = ordered[own, :]

    @pl.when(c == 1)
    def _():
        mate = shift_of(sibling)

        @pl.when((shift != 0) & (mate != 0))
        def _():
            pl.semaphore_wait(barrier, 2)

        @pl.when((shift == 0) | (mate == 0))
        def _():
            pl.semaphore_wait(barrier, 1)

        pl.semaphore_signal(far_sem, inc=1, device_id=(sibling, z), device_id_type=MESH)

    @pl.when(c == 0)
    def _():
        pl.semaphore_wait(far_sem, 1)

    wait_bytes(land.at[pl.ds(0, (N - 1) * rows), :], recv_sem.at[0])
    acc = land[pl.ds(0, rows), :].astype(jnp.float32)
    for k in range(1, N):
        acc = acc + land[pl.ds(k * rows, rows), :].astype(jnp.float32)
    slab = acc.astype(jnp.bfloat16)
    came = slab_of(down)

    @pl.when(shift == 0)
    def _():
        gfull[came, :] = slab

    @pl.when(shift != 0)
    def _():
        summed[...] = slab
        remote(summed, gfull.at[slab_of(z), :], 1, r, up).start()

    loads[2].wait()
    for step in PEERS:
        remote(lfull.at[own, :], lfull.at[own, :], 2, peer_of(step), z).start()
    loads[3].wait()
    loads[4].wait()
    holder = rep_of((z + NZ - r) % NZ)

    @pl.when(holder == r)
    def _():
        moments_land[...] = moments_v[...]

    @pl.when(holder != r)
    def _():
        remote(moments_v, moments_land, 3, holder, z).start()
        wait_bytes(moments_v, recv_sem.at[3])

    @pl.when(shift != 0)
    def _():
        wait_bytes(summed, recv_sem.at[1])

    is_late = (down // 16) * (1 - (down // 8) % 2)
    for step in PEERS:
        pltpu.make_async_remote_copy(
            src_ref=gfull.at[came, :],
            dst_ref=gfull.at[came, :],
            send_sem=send_sem.at[4],
            recv_sem=slab_sem.at[is_late],
            device_id=(peer_of(step), z),
            device_id_type=MESH,
        ).start()

    def blend(moments, grad):
        one = 0.9 * moments[0] + 0.1 * grad
        two = 0.95 * moments[1] + 0.05 * grad * grad
        return one, two

    def fold(v):
        v = v * v
        v = sum(v[:, 128 * k : 128 * (k + 1)] for k in range(v.shape[1] // 128))
        return jnp.sum(v, axis=0, keepdims=True)

    one, two = blend(moments_land[...], gfull[came, :].astype(jnp.float32))
    adam_part = fold(one / (jnp.sqrt(two) + 1e-08))
    sums_v[...] = adam_part
    sums_land[r] = adam_part
    for step in PEERS:
        remote(sums_v, sums_land.at[r], 5, peer_of(step), z).start()

    for load in loads[5:]:
        load.wait()
    wait_bytes(lfull.at[pl.ds(0, (N - 1) * rows), :], recv_sem.at[2])

    def wait_slabs(count, late):
        @pl.when(is_late == late)
        def _():
            wait_bytes(gfull.at[pl.ds(0, (count - 1) * rows), :], slab_sem.at[late])

        @pl.when(is_late != late)
        def _():
            wait_bytes(gfull.at[pl.ds(0, count * rows), :], slab_sem.at[late])

    wide = 128
    first = r * rows
    window = pl.ds(pl.multiple_of((first // wide) * wide, wide), wide)
    at = lax.broadcasted_iota(jnp.int32, (rows, wide), 1)
    want = lax.broadcasted_iota(jnp.int32, (rows, wide), 0) + first % wide
    pick = jnp.where(at == want, 1.0, 0.0).astype(jnp.bfloat16)

    def half_part(ks):
        return jnp.dot(lfull[:, ks], gfull[ks, :], preferred_element_type=jnp.float32)

    def right_part(ks):
        cols = lax.dot_general(pick, gfull[ks, window], NT, preferred_element_type=jnp.float32)
        return jnp.dot(cols.astype(jnp.bfloat16), gfull[ks, :], preferred_element_type=jnp.float32)

    early = (pl.ds(0, 256), pl.ds(384, 128))
    late = pl.ds(256, 128)
    wait_slabs(N - 8, 0)
    pre_v[...] = half_part(early[0]) + half_part(early[1])
    right_gram = right_part(early[0]) + right_part(early[1])
    wait_bytes(land.at[pl.ds(0, (N - 1) * rows), :], send_sem.at[0])

    @pl.when(shift != 0)
    def _():
        wait_bytes(summed, send_sem.at[1])

    wait_bytes(lfull.at[pl.ds(0, (N - 1) * rows), :], send_sem.at[2])

    @pl.when(holder != r)
    def _():
        wait_bytes(moments_v, send_sem.at[3])

    wait_slabs(8, 1)
    half_v[...] = (pre_v[...] + half_part(late)).astype(jnp.bfloat16)
    pre_part = jnp.zeros((1, 128), jnp.float32)
    for k in range(total_rows // chunk):
        part = pl.ds(k * chunk, chunk)
        precond = jnp.dot(half_v[part, :], rroot_v[...], preferred_element_type=jnp.float32)
        pre_v[part, :] = precond
        pre_part = pre_part + fold(precond)
    gram = lax.dot_general(gfull[own, :], gfull[...], NT, preferred_element_type=jnp.float32)
    left_ref[...] = 0.9 * sleft_v[...] + 0.1 * gram
    right_ref[...] = 0.9 * sright_v[...] + 0.1 * (right_gram + right_part(late))
    one, two = blend(moments_v[...], gfull[own, :].astype(jnp.float32))
    one_ref[...] = one
    two_ref[...] = two
    pre_sum = jnp.sum(pre_part, axis=1, keepdims=True)

    wait_bytes(sums_land.at[pl.ds(0, N - 1)], recv_sem.at[5])
    adam_sum = jnp.sum(jnp.sum(sums_land[...], axis=0), axis=1, keepdims=True)
    update_ref[...] = jnp.sqrt(adam_sum / (pre_sum + 1e-06)) * pre_v[own, :]
    wait_bytes(gfull.at[pl.ds(0, (N - 1) * rows), :], send_sem.at[4])
    wait_bytes(sums_land.at[pl.ds(0, N - 1)], send_sem.at[5])


def store_kernel(*refs):
    half = len(refs) // 2
    for src, dst in zip(refs[:half], refs[half:]):
        dst[...] = src[...]


def on_device(
    grad_partial,
    owner_slot,
    left_root,
    right_root,
    stat_left,
    stat_right,
    first_moment,
    second_moment,
):
    _, rows, nb, b = grad_partial.shape
    f32, bf16 = jnp.float32, jnp.bfloat16
    hbm = pl.BlockSpec(memory_space=pltpu.HBM)
    vmem = pl.BlockSpec(memory_space=pltpu.VMEM)
    shapes = [jax.ShapeDtypeStruct((rows, b), f32)] * 5
    outs = pl.pallas_call(
        step_kernel,
        out_shape=shapes,
        in_specs=[hbm] * 8,
        out_specs=[vmem] * 5,
        scratch_shapes=[
            pltpu.SMEM((nb,), jnp.int32),
            pltpu.VMEM((rows * nb, b), bf16),
            pltpu.VMEM((rows * nb, b), bf16),
            pltpu.VMEM((rows * N, b), bf16),
            pltpu.VMEM((rows, b), bf16),
            pltpu.VMEM((b, b), bf16),
            pltpu.VMEM((b, b), bf16),
            pltpu.VMEM((b, b), bf16),
            pltpu.VMEM((rows, b), f32),
            pltpu.VMEM((rows, b), f32),
            pltpu.VMEM((2, rows, b), f32),
            pltpu.VMEM((2, rows, b), f32),
            pltpu.VMEM((b, b), bf16),
            pltpu.VMEM((b, b), f32),
            pltpu.VMEM((1, 128), f32),
            pltpu.VMEM((N, 1, 128), f32),
            pltpu.SemaphoreType.DMA((8,)),
            pltpu.SemaphoreType.DMA((6,)),
            pltpu.SemaphoreType.DMA((6,)),
            pltpu.SemaphoreType.DMA((2,)),
            pltpu.SemaphoreType.REGULAR,
            pltpu.SemaphoreType.REGULAR,
        ],
        compiler_params=pltpu.CompilerParams(
            collective_id=0, has_side_effects=True, vmem_limit_bytes=32 * 1024 * 1024
        ),
        name="shampoo_step",
    )(
        *[
            pltpu.with_memory_space_constraint(v, pltpu.HBM)
            for v in (
                owner_slot,
                grad_partial.reshape(rows * nb, b),
                left_root[0],
                right_root[0],
                stat_left[0],
                stat_right[0],
                first_moment[0],
                second_moment[0],
            )
        ]
    )
    outs = pl.pallas_call(
        store_kernel,
        out_shape=shapes,
        in_specs=[vmem] * 5,
        out_specs=[vmem] * 5,
        compiler_params=pltpu.CompilerParams(vmem_limit_bytes=4 * 1024 * 1024),
        name="store_results",
    )(*outs)
    return tuple(out[None] for out in outs)


def solution(mesh):
    in_specs = (
        P("rep", "blk", None, None),
        P(),
        P("blk", "rep", None),
        P("blk", None, None),
        P("blk", "rep", None),
        P("blk", "rep", None),
        P("blk", "rep", None),
        P("blk", "rep", None),
    )
    out_specs = (P("blk", "rep", None),) * 5
    return jax.shard_map(
        on_device, mesh=mesh, in_specs=in_specs, out_specs=out_specs, check_vma=False
    )
```

```python
import jax
import jax.numpy as jnp
from jax import lax
from jax.experimental import pallas as pl
from jax.experimental.pallas import tpu as pltpu
from jax.sharding import PartitionSpec as P

MESH = pl.DeviceIdType.MESH
NX, NY, NC, NZ = 4, 4, 2, 32
N = NX * NY * NC
NT = (((1,), (1,)), ((), ()))


HALF = N // NC


def chip_distance(step):
    return min(step[0], NX - step[0]) + min(step[1], NY - step[1])


CHIPS = [(dx, dy) for dx in range(NX) for dy in range(NY)]
PEERS = sorted(
    [(dx, dy, dc) for dx, dy in CHIPS for dc in range(NC) if dx or dy or dc],
    key=chip_distance,
    reverse=True,
)


SAME = [(dx, dy) for dx, dy, dc in PEERS if dc == 0]

FAR = (0, 1, 2, 7, 4, 5, 6, 3)
NEAR = (1, 0, 3, 2, 5, 4, 7, 6)


def entry(table, k):
    value = table[0] + 0 * k
    for i in range(1, len(table)):
        value = jnp.where(k == i, table[i], value)
    return value


def rep_of(shift):
    high = shift // 16
    rank = high * (2 * (shift - 16)) + (1 - high) * (2 * (15 - shift) + 1)
    tier, k = rank // 8, rank % 8
    near, odd = tier // 2, tier % 2
    core = 1 - near
    j = core * entry(FAR, k) + near * entry(NEAR, k)
    x = j // 2
    y = 2 * (j % 2) + (odd + x) % 2
    return (x * NY + y) * NC + core


def shift_of(rep):
    x, y, core = rep // (NY * NC), (rep // NC) % NY, rep % NC
    j = x * 2 + y // 2
    far = entry([FAR.index(i) for i in range(8)], j)
    near = entry([NEAR.index(i) for i in range(8)], j)
    rank = (2 * (1 - core) + (x + y) % 2) * 8 + core * far + (1 - core) * near
    odd = rank % 2
    return (1 - odd) * (16 + rank // 2) + odd * (15 - rank // 2)


def shift_at(k, near):
    return 16 + k // 2 + 8 * near if k % 2 == 0 else 15 - k // 2 - 8 * near


def step_kernel(
    owner_hbm,
    grad_hbm,
    lroot_hbm,
    rroot_hbm,
    sleft_hbm,
    sright_hbm,
    mone_hbm,
    mtwo_hbm,
    update_ref,
    left_ref,
    right_ref,
    one_ref,
    two_ref,
    owner_s,
    grad_v,
    ordered,
    land,
    summed,
    gfull,
    lfull,
    rroot_v,
    sleft_v,
    sright_v,
    moments_v,
    moments_land,
    half_v,
    pre_v,
    sums_v,
    sums_land,
    load_sem,
    send_sem,
    recv_sem,
    slab_sem,
    hand_sem,
    plane_sem,
    far_sem,
):
    r = lax.axis_index("rep")
    z = lax.axis_index("blk")
    rows = summed.shape[0]
    x, y, c = r // (NY * NC), (r // NC) % NY, r % NC
    shift = shift_of(r)
    up = (z + shift) % NZ
    down = (z + NZ - shift) % NZ
    sibling = r + 1 - 2 * c

    def peer_of(step):
        dx, dy, dc = step
        return (((x + dx) % NX) * NY + (y + dy) % NY) * NC + (c + dc) % NC

    def slab_of(index):
        return pl.ds(pl.multiple_of(index * rows, rows), rows)

    def remote(src, dst, k, rep, blk):
        return pltpu.make_async_remote_copy(
            src_ref=src,
            dst_ref=dst,
            send_sem=send_sem.at[k],
            recv_sem=recv_sem.at[k],
            device_id=(rep, blk),
            device_id_type=MESH,
        )

    def wait_bytes(ref, sem):
        pltpu.make_async_copy(ref, ref, sem).wait()

    own = slab_of(r)
    pairs = [
        (grad_hbm, grad_v),
        (owner_hbm, owner_s),
        (lroot_hbm, lfull.at[own, :]),
        (mone_hbm, moments_v.at[0]),
        (mtwo_hbm, moments_v.at[1]),
        (rroot_hbm, rroot_v),
        (sleft_hbm, sleft_v),
        (sright_hbm, sright_v),
    ]
    loads = [pltpu.make_async_copy(src, dst, load_sem.at[k]) for k, (src, dst) in enumerate(pairs)]
    loads[0].start()
    loads[1].start()

    barrier = pltpu.get_barrier_semaphore()
    for dx, dy in sorted(CHIPS, key=chip_distance, reverse=True):
        chip = peer_of((dx, dy, 0)) - c

        @pl.when(chip != r)
        def _():
            pl.semaphore_signal(barrier, inc=1, device_id=(chip, z), device_id_type=MESH)

    @pl.when(shift != 0)
    def _():
        pl.semaphore_signal(barrier, inc=1, device_id=(r - c + 1, down), device_id_type=MESH)

    for load in loads[2:]:
        load.start()

    total_rows = grad_v.shape[0]
    nb = total_rows // rows
    lane = lax.broadcasted_iota(jnp.int32, (1, total_rows), 1)
    loads[1].wait()
    target = jnp.zeros((1, total_rows), jnp.int32)
    for b in range(nb):
        target = jnp.where(lane % nb == b, owner_s[b], target)
    target = rep_of((target + (NZ - z)) % NZ) * rows + lane // nb
    loads[0].wait()
    chunk = 128
    for k in range(total_rows // chunk):
        row = lax.broadcasted_iota(jnp.int32, (chunk, total_rows), 0) + k * chunk
        pick = jnp.where(row == target, 1.0, 0.0).astype(jnp.bfloat16)
        part = jnp.dot(pick, grad_v[...], preferred_element_type=jnp.float32)
        ordered[pl.ds(k * chunk, chunk), :] = part.astype(jnp.bfloat16)

    @pl.when(c == 0)
    def _():
        pl.semaphore_wait(barrier, N - 1)
        pl.semaphore_signal(plane_sem, inc=1, device_id=(sibling, z), device_id_type=MESH)

    @pl.when(c == 1)
    def _():
        pl.semaphore_wait(plane_sem, 1)

    for tier in range(4):
        core, odd = 1 - tier // 2, tier % 2
        for dx, m in ((2, 1), (2, 0), (1, 1), (3, 1), (0, 1), (1, 0), (3, 0), (0, 0)):
            px = (x + dx) % NX
            py = (y + 2 * m + (odd + px + y) % 2) % NY
            peer = (px * NY + py) * NC + core

            @pl.when(peer != r)
            def _():
                remote(ordered.at[slab_of(peer), :], land.at[own, :], 0, peer, z).start()

    land[own, :] = ordered[own, :]

    @pl.when(c == 1)
    def _():
        mate = shift_of(sibling)

        @pl.when((shift != 0) & (mate != 0))
        def _():
            pl.semaphore_wait(barrier, 2)

        @pl.when((shift == 0) | (mate == 0))
        def _():
            pl.semaphore_wait(barrier, 1)

        pl.semaphore_signal(far_sem, inc=1, device_id=(sibling, z), device_id_type=MESH)

    @pl.when(c == 0)
    def _():
        pl.semaphore_wait(far_sem, 1)

    wait_bytes(land.at[pl.ds(0, (N - 1) * rows), :], recv_sem.at[0])
    acc = land[pl.ds(0, rows), :].astype(jnp.float32)
    for k in range(1, N):
        acc = acc + land[pl.ds(k * rows, rows), :].astype(jnp.float32)
    slab = acc.astype(jnp.bfloat16)
    came = slab_of(down)

    @pl.when(shift == 0)
    def _():
        gfull[came, :] = slab

    @pl.when(shift != 0)
    def _():
        summed[...] = slab
        remote(summed, gfull.at[slab_of(z), :], 1, r, up).start()

    loads[2].wait()
    for step in PEERS:
        remote(lfull.at[own, :], lfull.at[own, :], 2, peer_of(step), z).start()
    loads[3].wait()
    loads[4].wait()
    holder = rep_of((z + NZ - r) % NZ)

    @pl.when(holder == r)
    def _():
        moments_land[...] = moments_v[...]

    @pl.when(holder != r)
    def _():
        remote(moments_v, moments_land, 3, holder, z).start()
        wait_bytes(moments_v, recv_sem.at[3])

    @pl.when(shift != 0)
    def _():
        wait_bytes(summed, recv_sem.at[1])

    k_own = sum(jnp.where(down == (z + NZ - shift_at(k, 1 - c)) % NZ, k, 0) for k in range(HALF))
    piece = gfull.at[came, :]
    for dx, dy in SAME:
        pltpu.make_async_remote_copy(
            src_ref=piece,
            dst_ref=piece,
            send_sem=send_sem.at[4],
            recv_sem=slab_sem.at[k_own],
            device_id=(peer_of((dx, dy, 0)), z),
            device_id_type=MESH,
        ).start()

    def hand_over(piece, k):
        pltpu.make_async_remote_copy(
            src_ref=piece,
            dst_ref=piece,
            send_sem=send_sem.at[6],
            recv_sem=hand_sem.at[k],
            device_id=(sibling, z),
            device_id_type=MESH,
        ).start()

    hand_over(piece, k_own)

    def blend(moments, grad):
        one = 0.9 * moments[0] + 0.1 * grad
        two = 0.95 * moments[1] + 0.05 * grad * grad
        return one, two

    def fold(v):
        v = v * v
        v = sum(v[:, 128 * k : 128 * (k + 1)] for k in range(v.shape[1] // 128))
        return jnp.sum(v, axis=0, keepdims=True)

    one, two = blend(moments_land[...], gfull[came, :].astype(jnp.float32))
    adam_part = fold(one / (jnp.sqrt(two) + 1e-08))
    sums_v[...] = adam_part
    sums_land[r] = adam_part
    for step in PEERS:
        remote(sums_v, sums_land.at[r], 5, peer_of(step), z).start()

    for load in loads[5:]:
        load.wait()
    wait_bytes(lfull.at[pl.ds(0, (N - 1) * rows), :], recv_sem.at[2])

    def wait_slabs(late):
        for k in reversed(range(HALF)):
            plane = (z + NZ - shift_at(k, 1 - c)) % NZ

            @pl.when(((plane // 8 == 2) == late) & (k_own != k))
            def _():
                piece = gfull.at[slab_of(plane), :]
                wait_bytes(piece, slab_sem.at[k])
                hand_over(piece, k)

        for k in reversed(range(HALF)):
            plane = (z + NZ - shift_at(k, c)) % NZ

            @pl.when((plane // 8 == 2) == late)
            def _():
                wait_bytes(gfull.at[slab_of(plane), :], hand_sem.at[k])

    wide = 128
    first = r * rows
    window = pl.ds(pl.multiple_of((first // wide) * wide, wide), wide)
    at = lax.broadcasted_iota(jnp.int32, (rows, wide), 1)
    want = lax.broadcasted_iota(jnp.int32, (rows, wide), 0) + first % wide
    pick = jnp.where(at == want, 1.0, 0.0).astype(jnp.bfloat16)

    def half_part(ks):
        return jnp.dot(lfull[:, ks], gfull[ks, :], preferred_element_type=jnp.float32)

    def right_part(ks):
        cols = lax.dot_general(pick, gfull[ks, window], NT, preferred_element_type=jnp.float32)
        return jnp.dot(cols.astype(jnp.bfloat16), gfull[ks, :], preferred_element_type=jnp.float32)

    early = (pl.ds(0, 256), pl.ds(384, 128))
    late = pl.ds(256, 128)
    wait_slabs(False)
    pre_v[...] = half_part(early[0]) + half_part(early[1])
    right_gram = right_part(early[0]) + right_part(early[1])
    wait_bytes(land.at[pl.ds(0, (N - 1) * rows), :], send_sem.at[0])

    @pl.when(shift != 0)
    def _():
        wait_bytes(summed, send_sem.at[1])

    wait_bytes(lfull.at[pl.ds(0, (N - 1) * rows), :], send_sem.at[2])

    @pl.when(holder != r)
    def _():
        wait_bytes(moments_v, send_sem.at[3])

    wait_slabs(True)
    half_v[...] = (pre_v[...] + half_part(late)).astype(jnp.bfloat16)
    pre_part = jnp.zeros((1, 128), jnp.float32)
    for k in range(total_rows // chunk):
        part = pl.ds(k * chunk, chunk)
        precond = jnp.dot(half_v[part, :], rroot_v[...], preferred_element_type=jnp.float32)
        pre_v[part, :] = precond
        pre_part = pre_part + fold(precond)
    gram = lax.dot_general(gfull[own, :], gfull[...], NT, preferred_element_type=jnp.float32)
    left_ref[...] = 0.9 * sleft_v[...] + 0.1 * gram
    right_ref[...] = 0.9 * sright_v[...] + 0.1 * (right_gram + right_part(late))
    one, two = blend(moments_v[...], gfull[own, :].astype(jnp.float32))
    one_ref[...] = one
    two_ref[...] = two
    pre_sum = jnp.sum(pre_part, axis=1, keepdims=True)

    wait_bytes(sums_land.at[pl.ds(0, N - 1)], recv_sem.at[5])
    adam_sum = jnp.sum(jnp.sum(sums_land[...], axis=0), axis=1, keepdims=True)
    update_ref[...] = jnp.sqrt(adam_sum / (pre_sum + 1e-06)) * pre_v[own, :]
    wait_bytes(gfull.at[pl.ds(0, (HALF - 1) * rows), :], send_sem.at[4])
    wait_bytes(gfull.at[pl.ds(0, HALF * rows), :], send_sem.at[6])
    wait_bytes(sums_land.at[pl.ds(0, N - 1)], send_sem.at[5])


def store_kernel(*refs):
    half = len(refs) // 2
    for src, dst in zip(refs[:half], refs[half:]):
        dst[...] = src[...]


def on_device(
    grad_partial,
    owner_slot,
    left_root,
    right_root,
    stat_left,
    stat_right,
    first_moment,
    second_moment,
):
    _, rows, nb, b = grad_partial.shape
    f32, bf16 = jnp.float32, jnp.bfloat16
    hbm = pl.BlockSpec(memory_space=pltpu.HBM)
    vmem = pl.BlockSpec(memory_space=pltpu.VMEM)
    shapes = [jax.ShapeDtypeStruct((rows, b), f32)] * 5
    outs = pl.pallas_call(
        step_kernel,
        out_shape=shapes,
        in_specs=[hbm] * 8,
        out_specs=[vmem] * 5,
        scratch_shapes=[
            pltpu.SMEM((nb,), jnp.int32),
            pltpu.VMEM((rows * nb, b), bf16),
            pltpu.VMEM((rows * nb, b), bf16),
            pltpu.VMEM((rows * N, b), bf16),
            pltpu.VMEM((rows, b), bf16),
            pltpu.VMEM((b, b), bf16),
            pltpu.VMEM((b, b), bf16),
            pltpu.VMEM((b, b), bf16),
            pltpu.VMEM((rows, b), f32),
            pltpu.VMEM((rows, b), f32),
            pltpu.VMEM((2, rows, b), f32),
            pltpu.VMEM((2, rows, b), f32),
            pltpu.VMEM((b, b), bf16),
            pltpu.VMEM((b, b), f32),
            pltpu.VMEM((1, 128), f32),
            pltpu.VMEM((N, 1, 128), f32),
            pltpu.SemaphoreType.DMA((8,)),
            pltpu.SemaphoreType.DMA((7,)),
            pltpu.SemaphoreType.DMA((6,)),
            pltpu.SemaphoreType.DMA((HALF,)),
            pltpu.SemaphoreType.DMA((HALF,)),
            pltpu.SemaphoreType.REGULAR,
            pltpu.SemaphoreType.REGULAR,
        ],
        compiler_params=pltpu.CompilerParams(
            collective_id=0, has_side_effects=True, vmem_limit_bytes=32 * 1024 * 1024
        ),
        name="shampoo_step",
    )(
        *[
            pltpu.with_memory_space_constraint(v, pltpu.HBM)
            for v in (
                owner_slot,
                grad_partial.reshape(rows * nb, b),
                left_root[0],
                right_root[0],
                stat_left[0],
                stat_right[0],
                first_moment[0],
                second_moment[0],
            )
        ]
    )
    outs = pl.pallas_call(
        store_kernel,
        out_shape=shapes,
        in_specs=[vmem] * 5,
        out_specs=[vmem] * 5,
        compiler_params=pltpu.CompilerParams(vmem_limit_bytes=4 * 1024 * 1024),
        name="store_results",
    )(*outs)
    return tuple(out[None] for out in outs)


def solution(mesh):
    in_specs = (
        P("rep", "blk", None, None),
        P(),
        P("blk", "rep", None),
        P("blk", None, None),
        P("blk", "rep", None),
        P("blk", "rep", None),
        P("blk", "rep", None),
        P("blk", "rep", None),
    )
    out_specs = (P("blk", "rep", None),) * 5
    return jax.shard_map(
        on_device, mesh=mesh, in_specs=in_specs, out_specs=out_specs, check_vma=False
    )
```

```python
import jax
import jax.numpy as jnp
from jax import lax
from jax.experimental import pallas as pl
from jax.experimental.pallas import tpu as pltpu
from jax.sharding import PartitionSpec as P

MESH = pl.DeviceIdType.MESH
NX, NY, NC, NZ = 4, 4, 2, 32
N = NX * NY * NC
NT = (((1,), (1,)), ((), ()))


HALF = N // NC


def chip_distance(step):
    return min(step[0], NX - step[0]) + min(step[1], NY - step[1])


CHIPS = [(dx, dy) for dx in range(NX) for dy in range(NY)]
PEERS = sorted(
    [(dx, dy, dc) for dx, dy in CHIPS for dc in range(NC) if dx or dy or dc],
    key=chip_distance,
    reverse=True,
)


SAME = [(dx, dy) for dx, dy, dc in PEERS if dc == 0]

FAR = (0, 1, 2, 7, 4, 5, 3, 6)
NEAR = (1, 0, 3, 2, 5, 4, 7, 6)


def entry(table, k):
    value = table[0] + 0 * k
    for i in range(1, len(table)):
        value = jnp.where(k == i, table[i], value)
    return value


def rep_of(shift):
    high = shift // 16
    rank = high * (2 * (shift - 16)) + (1 - high) * (2 * (15 - shift) + 1)
    tier, k = rank // 8, rank % 8
    near, odd = tier // 2, tier % 2
    core = 1 - near
    j = core * entry(FAR, k) + near * entry(NEAR, k)
    x = j // 2
    y = 2 * (j % 2) + (odd + x) % 2
    return (x * NY + y) * NC + core


def shift_of(rep):
    x, y, core = rep // (NY * NC), (rep // NC) % NY, rep % NC
    j = x * 2 + y // 2
    far = entry([FAR.index(i) for i in range(8)], j)
    near = entry([NEAR.index(i) for i in range(8)], j)
    rank = (2 * (1 - core) + (x + y) % 2) * 8 + core * far + (1 - core) * near
    odd = rank % 2
    return (1 - odd) * (16 + rank // 2) + odd * (15 - rank // 2)


def shift_at(k, near):
    return 16 + k // 2 + 8 * near if k % 2 == 0 else 15 - k // 2 - 8 * near


def step_kernel(
    owner_hbm,
    grad_hbm,
    lroot_hbm,
    rroot_hbm,
    sleft_hbm,
    sright_hbm,
    mone_hbm,
    mtwo_hbm,
    update_ref,
    left_ref,
    right_ref,
    one_ref,
    two_ref,
    owner_s,
    grad_v,
    ordered,
    land,
    summed,
    gfull,
    lfull,
    rroot_v,
    sleft_v,
    sright_v,
    moments_v,
    moments_land,
    half_v,
    pre_v,
    sums_v,
    sums_land,
    load_sem,
    send_sem,
    recv_sem,
    slab_sem,
    hand_sem,
    plane_sem,
    far_sem,
):
    r = lax.axis_index("rep")
    z = lax.axis_index("blk")
    rows = summed.shape[0]
    x, y, c = r // (NY * NC), (r // NC) % NY, r % NC
    shift = shift_of(r)
    up = (z + shift) % NZ
    down = (z + NZ - shift) % NZ
    sibling = r + 1 - 2 * c

    def peer_of(step):
        dx, dy, dc = step
        return (((x + dx) % NX) * NY + (y + dy) % NY) * NC + (c + dc) % NC

    def slab_of(index):
        return pl.ds(pl.multiple_of(index * rows, rows), rows)

    def remote(src, dst, k, rep, blk):
        return pltpu.make_async_remote_copy(
            src_ref=src,
            dst_ref=dst,
            send_sem=send_sem.at[k],
            recv_sem=recv_sem.at[k],
            device_id=(rep, blk),
            device_id_type=MESH,
        )

    def wait_bytes(ref, sem):
        pltpu.make_async_copy(ref, ref, sem).wait()

    own = slab_of(r)
    pairs = [
        (grad_hbm, grad_v),
        (owner_hbm, owner_s),
        (lroot_hbm, lfull.at[own, :]),
        (mone_hbm, moments_v.at[0]),
        (mtwo_hbm, moments_v.at[1]),
        (rroot_hbm, rroot_v),
        (sleft_hbm, sleft_v),
        (sright_hbm, sright_v),
    ]
    loads = [pltpu.make_async_copy(src, dst, load_sem.at[k]) for k, (src, dst) in enumerate(pairs)]
    loads[0].start()
    loads[1].start()

    barrier = pltpu.get_barrier_semaphore()
    for dx, dy in sorted(CHIPS, key=chip_distance, reverse=True):
        chip = peer_of((dx, dy, 0)) - c

        @pl.when(chip != r)
        def _():
            pl.semaphore_signal(barrier, inc=1, device_id=(chip, z), device_id_type=MESH)

    @pl.when(shift != 0)
    def _():
        pl.semaphore_signal(barrier, inc=1, device_id=(r - c + 1, down), device_id_type=MESH)

    for load in loads[2:]:
        load.start()

    total_rows = grad_v.shape[0]
    nb = total_rows // rows
    lane = lax.broadcasted_iota(jnp.int32, (1, total_rows), 1)
    loads[1].wait()
    target = jnp.zeros((1, total_rows), jnp.int32)
    for b in range(nb):
        target = jnp.where(lane % nb == b, owner_s[b], target)
    target = rep_of((target + (NZ - z)) % NZ) * rows + lane // nb
    loads[0].wait()
    chunk = 128
    for k in range(total_rows // chunk):
        row = lax.broadcasted_iota(jnp.int32, (chunk, total_rows), 0) + k * chunk
        pick = jnp.where(row == target, 1.0, 0.0).astype(jnp.bfloat16)
        part = jnp.dot(pick, grad_v[...], preferred_element_type=jnp.float32)
        ordered[pl.ds(k * chunk, chunk), :] = part.astype(jnp.bfloat16)

    @pl.when(c == 0)
    def _():
        pl.semaphore_wait(barrier, N - 1)
        pl.semaphore_signal(plane_sem, inc=1, device_id=(sibling, z), device_id_type=MESH)

    @pl.when(c == 1)
    def _():
        pl.semaphore_wait(plane_sem, 1)

    for tier in range(4):
        core, odd = 1 - tier // 2, tier % 2
        for dx, m in ((2, 1), (2, 0), (1, 1), (3, 1), (0, 1), (1, 0), (3, 0), (0, 0)):
            px = (x + dx) % NX
            py = (y + 2 * m + (odd + px + y) % 2) % NY
            peer = (px * NY + py) * NC + core

            @pl.when(peer != r)
            def _():
                remote(ordered.at[slab_of(peer), :], land.at[own, :], 0, peer, z).start()

    land[own, :] = ordered[own, :]

    @pl.when(c == 1)
    def _():
        mate = shift_of(sibling)

        @pl.when((shift != 0) & (mate != 0))
        def _():
            pl.semaphore_wait(barrier, 2)

        @pl.when((shift == 0) | (mate == 0))
        def _():
            pl.semaphore_wait(barrier, 1)

        pl.semaphore_signal(far_sem, inc=1, device_id=(sibling, z), device_id_type=MESH)

    @pl.when(c == 0)
    def _():
        pl.semaphore_wait(far_sem, 1)

    wait_bytes(land.at[pl.ds(0, (N - 1) * rows), :], recv_sem.at[0])
    acc = land[pl.ds(0, rows), :].astype(jnp.float32)
    for k in range(1, N):
        acc = acc + land[pl.ds(k * rows, rows), :].astype(jnp.float32)
    slab = acc.astype(jnp.bfloat16)
    came = slab_of(down)

    @pl.when(shift == 0)
    def _():
        gfull[came, :] = slab

    @pl.when(shift != 0)
    def _():
        summed[...] = slab
        remote(summed, gfull.at[slab_of(z), :], 1, r, up).start()

    loads[2].wait()
    for step in PEERS:
        remote(lfull.at[own, :], lfull.at[own, :], 2, peer_of(step), z).start()
    loads[3].wait()
    loads[4].wait()
    holder = rep_of((z + NZ - r) % NZ)

    @pl.when(holder == r)
    def _():
        moments_land[...] = moments_v[...]

    @pl.when(holder != r)
    def _():
        remote(moments_v, moments_land, 3, holder, z).start()
        wait_bytes(moments_v, recv_sem.at[3])

    @pl.when(shift != 0)
    def _():
        wait_bytes(summed, recv_sem.at[1])

    k_own = sum(jnp.where(down == (z + NZ - shift_at(k, 1 - c)) % NZ, k, 0) for k in range(HALF))
    piece = gfull.at[came, :]
    for dx, dy in SAME:
        pltpu.make_async_remote_copy(
            src_ref=piece,
            dst_ref=piece,
            send_sem=send_sem.at[4],
            recv_sem=slab_sem.at[k_own],
            device_id=(peer_of((dx, dy, 0)), z),
            device_id_type=MESH,
        ).start()

    def hand_over(piece, k):
        pltpu.make_async_remote_copy(
            src_ref=piece,
            dst_ref=piece,
            send_sem=send_sem.at[6],
            recv_sem=hand_sem.at[k],
            device_id=(sibling, z),
            device_id_type=MESH,
        ).start()

    hand_over(piece, k_own)

    def blend(moments, grad):
        one = 0.9 * moments[0] + 0.1 * grad
        two = 0.95 * moments[1] + 0.05 * grad * grad
        return one, two

    def fold(v):
        v = v * v
        v = sum(v[:, 128 * k : 128 * (k + 1)] for k in range(v.shape[1] // 128))
        return jnp.sum(v, axis=0, keepdims=True)

    one, two = blend(moments_land[...], gfull[came, :].astype(jnp.float32))
    adam_part = fold(one / (jnp.sqrt(two) + 1e-08))
    sums_v[...] = adam_part
    sums_land[r] = adam_part
    for step in PEERS:
        remote(sums_v, sums_land.at[r], 5, peer_of(step), z).start()

    for load in loads[5:]:
        load.wait()
    wait_bytes(lfull.at[pl.ds(0, (N - 1) * rows), :], recv_sem.at[2])

    def wait_slabs(late):
        for k in reversed(range(HALF)):
            plane = (z + NZ - shift_at(k, 1 - c)) % NZ

            @pl.when(((plane // 8 == 2) == late) & (k_own != k))
            def _():
                piece = gfull.at[slab_of(plane), :]
                wait_bytes(piece, slab_sem.at[k])
                hand_over(piece, k)

        for k in reversed(range(HALF)):
            plane = (z + NZ - shift_at(k, c)) % NZ

            @pl.when((plane // 8 == 2) == late)
            def _():
                wait_bytes(gfull.at[slab_of(plane), :], hand_sem.at[k])

    wide = 128
    first = r * rows
    window = pl.ds(pl.multiple_of((first // wide) * wide, wide), wide)
    at = lax.broadcasted_iota(jnp.int32, (rows, wide), 1)
    want = lax.broadcasted_iota(jnp.int32, (rows, wide), 0) + first % wide
    pick = jnp.where(at == want, 1.0, 0.0).astype(jnp.bfloat16)

    def half_part(ks):
        return jnp.dot(lfull[:, ks], gfull[ks, :], preferred_element_type=jnp.float32)

    def right_part(ks):
        cols = lax.dot_general(pick, gfull[ks, window], NT, preferred_element_type=jnp.float32)
        return jnp.dot(cols.astype(jnp.bfloat16), gfull[ks, :], preferred_element_type=jnp.float32)

    early = (pl.ds(0, 256), pl.ds(384, 128))
    late = pl.ds(256, 128)
    wait_slabs(False)
    pre_v[...] = half_part(early[0]) + half_part(early[1])
    right_gram = right_part(early[0]) + right_part(early[1])
    wait_bytes(land.at[pl.ds(0, (N - 1) * rows), :], send_sem.at[0])

    @pl.when(shift != 0)
    def _():
        wait_bytes(summed, send_sem.at[1])

    wait_bytes(lfull.at[pl.ds(0, (N - 1) * rows), :], send_sem.at[2])

    @pl.when(holder != r)
    def _():
        wait_bytes(moments_v, send_sem.at[3])

    wait_slabs(True)
    half_v[...] = (pre_v[...] + half_part(late)).astype(jnp.bfloat16)
    pre_part = jnp.zeros((1, 128), jnp.float32)
    for k in range(total_rows // chunk):
        part = pl.ds(k * chunk, chunk)
        precond = jnp.dot(half_v[part, :], rroot_v[...], preferred_element_type=jnp.float32)
        pre_v[part, :] = precond
        pre_part = pre_part + fold(precond)
    gram = lax.dot_general(gfull[own, :], gfull[...], NT, preferred_element_type=jnp.float32)
    left_ref[...] = 0.9 * sleft_v[...] + 0.1 * gram
    right_ref[...] = 0.9 * sright_v[...] + 0.1 * (right_gram + right_part(late))
    one, two = blend(moments_v[...], gfull[own, :].astype(jnp.float32))
    one_ref[...] = one
    two_ref[...] = two
    pre_sum = jnp.sum(pre_part, axis=1, keepdims=True)

    wait_bytes(sums_land.at[pl.ds(0, N - 1)], recv_sem.at[5])
    adam_sum = jnp.sum(jnp.sum(sums_land[...], axis=0), axis=1, keepdims=True)
    update_ref[...] = jnp.sqrt(adam_sum / (pre_sum + 1e-06)) * pre_v[own, :]
    wait_bytes(gfull.at[pl.ds(0, (HALF - 1) * rows), :], send_sem.at[4])
    wait_bytes(gfull.at[pl.ds(0, HALF * rows), :], send_sem.at[6])
    wait_bytes(sums_land.at[pl.ds(0, N - 1)], send_sem.at[5])


def store_kernel(*refs):
    half = len(refs) // 2
    for src, dst in zip(refs[:half], refs[half:]):
        dst[...] = src[...]


def on_device(
    grad_partial,
    owner_slot,
    left_root,
    right_root,
    stat_left,
    stat_right,
    first_moment,
    second_moment,
):
    _, rows, nb, b = grad_partial.shape
    f32, bf16 = jnp.float32, jnp.bfloat16
    hbm = pl.BlockSpec(memory_space=pltpu.HBM)
    vmem = pl.BlockSpec(memory_space=pltpu.VMEM)
    shapes = [jax.ShapeDtypeStruct((rows, b), f32)] * 5
    outs = pl.pallas_call(
        step_kernel,
        out_shape=shapes,
        in_specs=[hbm] * 8,
        out_specs=[vmem] * 5,
        scratch_shapes=[
            pltpu.SMEM((nb,), jnp.int32),
            pltpu.VMEM((rows * nb, b), bf16),
            pltpu.VMEM((rows * nb, b), bf16),
            pltpu.VMEM((rows * N, b), bf16),
            pltpu.VMEM((rows, b), bf16),
            pltpu.VMEM((b, b), bf16),
            pltpu.VMEM((b, b), bf16),
            pltpu.VMEM((b, b), bf16),
            pltpu.VMEM((rows, b), f32),
            pltpu.VMEM((rows, b), f32),
            pltpu.VMEM((2, rows, b), f32),
            pltpu.VMEM((2, rows, b), f32),
            pltpu.VMEM((b, b), bf16),
            pltpu.VMEM((b, b), f32),
            pltpu.VMEM((1, 128), f32),
            pltpu.VMEM((N, 1, 128), f32),
            pltpu.SemaphoreType.DMA((8,)),
            pltpu.SemaphoreType.DMA((7,)),
            pltpu.SemaphoreType.DMA((6,)),
            pltpu.SemaphoreType.DMA((HALF,)),
            pltpu.SemaphoreType.DMA((HALF,)),
            pltpu.SemaphoreType.REGULAR,
            pltpu.SemaphoreType.REGULAR,
        ],
        compiler_params=pltpu.CompilerParams(
            collective_id=0, has_side_effects=True, vmem_limit_bytes=32 * 1024 * 1024
        ),
        name="shampoo_step",
    )(
        *[
            pltpu.with_memory_space_constraint(v, pltpu.HBM)
            for v in (
                owner_slot,
                grad_partial.reshape(rows * nb, b),
                left_root[0],
                right_root[0],
                stat_left[0],
                stat_right[0],
                first_moment[0],
                second_moment[0],
            )
        ]
    )
    outs = pl.pallas_call(
        store_kernel,
        out_shape=shapes,
        in_specs=[vmem] * 5,
        out_specs=[vmem] * 5,
        compiler_params=pltpu.CompilerParams(vmem_limit_bytes=4 * 1024 * 1024),
        name="store_results",
    )(*outs)
    return tuple(out[None] for out in outs)


def solution(mesh):
    in_specs = (
        P("rep", "blk", None, None),
        P(),
        P("blk", "rep", None),
        P("blk", None, None),
        P("blk", "rep", None),
        P("blk", "rep", None),
        P("blk", "rep", None),
        P("blk", "rep", None),
    )
    out_specs = (P("blk", "rep", None),) * 5
    return jax.shard_map(
        on_device, mesh=mesh, in_specs=in_specs, out_specs=out_specs, check_vma=False
    )
```

```python
import functools

import jax
import jax.numpy as jnp
from jax import lax
from jax.experimental import pallas as pl
from jax.experimental.pallas import tpu as pltpu
from jax.sharding import PartitionSpec as P

MESH = pl.DeviceIdType.MESH
NX, NY, NC, NZ = 4, 4, 2, 32
N = NX * NY * NC
NT = (((1,), (1,)), ((), ()))


HALF = N // NC


def chip_distance(step):
    return min(step[0], NX - step[0]) + min(step[1], NY - step[1])


CHIPS = [(dx, dy) for dx in range(NX) for dy in range(NY)]
PEERS = sorted(
    [(dx, dy, dc) for dx, dy in CHIPS for dc in range(NC) if dx or dy or dc],
    key=chip_distance,
    reverse=True,
)


SAME = [(dx, dy) for dx, dy, dc in PEERS if dc == 0]

FAR = (0, 1, 2, 7, 4, 5, 3, 6)
NEAR = (1, 0, 3, 2, 5, 4, 7, 6)


def entry(table, k):
    value = table[0] + 0 * k
    for i in range(1, len(table)):
        value = jnp.where(k == i, table[i], value)
    return value


def rep_of(shift):
    high = shift // 16
    rank = high * (2 * (shift - 16)) + (1 - high) * (2 * (15 - shift) + 1)
    tier, k = rank // 8, rank % 8
    near, odd = tier // 2, tier % 2
    core = 1 - near
    j = core * entry(FAR, k) + near * entry(NEAR, k)
    x = j // 2
    y = 2 * (j % 2) + (odd + x) % 2
    return (x * NY + y) * NC + core


def shift_of(rep):
    x, y, core = rep // (NY * NC), (rep // NC) % NY, rep % NC
    j = x * 2 + y // 2
    far = entry([FAR.index(i) for i in range(8)], j)
    near = entry([NEAR.index(i) for i in range(8)], j)
    rank = (2 * (1 - core) + (x + y) % 2) * 8 + core * far + (1 - core) * near
    odd = rank % 2
    return (1 - odd) * (16 + rank // 2) + odd * (15 - rank // 2)


def shift_at(k, near):
    return 16 + k // 2 + 8 * near if k % 2 == 0 else 15 - k // 2 - 8 * near


def step_kernel(
    owner_hbm,
    grad_hbm,
    lroot_hbm,
    rroot_hbm,
    sleft_hbm,
    sright_hbm,
    mone_hbm,
    mtwo_hbm,
    update_ref,
    left_ref,
    right_ref,
    one_ref,
    two_ref,
    owner_s,
    grad_v,
    ordered,
    land,
    summed,
    gfull,
    lfull,
    rroot_v,
    sleft_v,
    sright_v,
    moments_v,
    moments_land,
    half_v,
    pre_v,
    sums_v,
    sums_land,
    load_sem,
    send_sem,
    recv_sem,
    slab_sem,
    hand_sem,
    plane_sem,
    far_sem,
):
    r = lax.axis_index("rep")
    z = lax.axis_index("blk")
    rows = summed.shape[0]
    x, y, c = r // (NY * NC), (r // NC) % NY, r % NC
    shift = shift_of(r)
    up = (z + shift) % NZ
    down = (z + NZ - shift) % NZ
    sibling = r + 1 - 2 * c

    def peer_of(step):
        dx, dy, dc = step
        return (lax.rem(x + dx, NX) * NY + lax.rem(y + dy, NY)) * NC + lax.rem(c + dc, NC)

    def slab_of(index):
        return pl.ds(pl.multiple_of(index * rows, rows), rows)

    def remote(src, dst, k, rep, blk):
        return pltpu.make_async_remote_copy(
            src_ref=src,
            dst_ref=dst,
            send_sem=send_sem.at[k],
            recv_sem=recv_sem.at[k],
            device_id=(rep, blk),
            device_id_type=MESH,
        )

    def wait_bytes(ref, sem):
        pltpu.make_async_copy(ref, ref, sem).wait()

    own = slab_of(r)
    pairs = [
        (grad_hbm, grad_v),
        (owner_hbm, owner_s),
        (lroot_hbm, lfull.at[own, :]),
        (mone_hbm, moments_v.at[0]),
        (mtwo_hbm, moments_v.at[1]),
        (rroot_hbm, rroot_v),
        (sleft_hbm, sleft_v),
        (sright_hbm, sright_v),
    ]
    loads = [pltpu.make_async_copy(src, dst, load_sem.at[k]) for k, (src, dst) in enumerate(pairs)]
    loads[0].start()
    loads[1].start()

    barrier = pltpu.get_barrier_semaphore()
    for dx, dy in sorted(CHIPS, key=chip_distance, reverse=True):
        chip = peer_of((dx, dy, 0)) - c
        if dx or dy:
            pl.semaphore_signal(barrier, inc=1, device_id=(chip, z), device_id_type=MESH)

    @pl.when(c == 1)
    def _():
        pl.semaphore_signal(barrier, inc=1, device_id=(sibling, z), device_id_type=MESH)

    @pl.when(shift != 0)
    def _():
        pl.semaphore_signal(barrier, inc=1, device_id=(r - c + 1, down), device_id_type=MESH)

    for load in loads[2:]:
        load.start()

    total_rows = grad_v.shape[0]
    nb = total_rows // rows
    lane = lax.broadcasted_iota(jnp.int32, (1, total_rows), 1)
    loads[1].wait()
    target = jnp.zeros((1, total_rows), jnp.int32)
    for b in range(nb):
        target = jnp.where(lane % nb == b, owner_s[b], target)
    target = rep_of((target + (NZ - z)) % NZ) * rows + lane // nb
    loads[0].wait()
    chunk = 128
    for k in range(total_rows // chunk):
        row = lax.broadcasted_iota(jnp.int32, (chunk, total_rows), 0) + k * chunk
        pick = jnp.where(row == target, 1.0, 0.0).astype(jnp.bfloat16)
        part = jnp.dot(pick, grad_v[...], preferred_element_type=jnp.float32)
        ordered[pl.ds(k * chunk, chunk), :] = part.astype(jnp.bfloat16)

    targets = []
    for tier in range(4):
        core, odd = 1 - tier // 2, tier % 2
        for dx, m in ((2, 1), (2, 0), (1, 1), (3, 1), (0, 1), (1, 0), (3, 0), (0, 0)):
            px = lax.rem(x + dx, NX)
            py = lax.rem(y + 2 * m + lax.rem(odd + px + y, 2), NY)
            targets.append((px * NY + py) * NC + core)
    peers = [peer_of(step) for step in PEERS]
    same = [peer_of((dx, dy, 0)) for dx, dy in SAME]

    first_hand = [lax.rem(z + NZ - shift_at(k, 1 - c), NZ) for k in range(HALF)]
    second_hand = [lax.rem(z + NZ - shift_at(k, c), NZ) for k in range(HALF)]
    k_own = sum(jnp.where(down == first_hand[k], k, 0) for k in range(HALF))

    @pl.when(c == 0)
    def _():
        pl.semaphore_wait(barrier, N - 1)
        pl.semaphore_signal(plane_sem, inc=1, device_id=(sibling, z), device_id_type=MESH)

    @pl.when(c == 1)
    def _():
        pl.semaphore_wait(plane_sem, 1)

    def scatter_to(peer):
        remote(ordered.at[slab_of(peer), :], land.at[own, :], 0, peer, z).start()

    def is_above(peer):
        j = 2 * lax.div(peer, NY * NC) + lax.rem(lax.div(peer, 2 * NC), 2)
        return (j < 2) | (j > 4)

    above = [is_above(peer) for peer in targets[:8]]
    for peer, up_first in zip(targets[:8], above):
        pl.when((peer != r) & up_first)(functools.partial(scatter_to, peer))
    for peer, up_first in zip(targets[:8], above):
        pl.when((peer != r) & jnp.logical_not(up_first))(functools.partial(scatter_to, peer))
    for i, peer in enumerate(targets[8:]):
        if i % 8 < 7:
            scatter_to(peer)
        else:
            pl.when(peer != r)(functools.partial(scatter_to, peer))

    land[own, :] = ordered[own, :]

    @pl.when(c == 1)
    def _():
        mate = shift_of(sibling)

        @pl.when((shift != 0) & (mate != 0))
        def _():
            pl.semaphore_wait(barrier, 2)

        @pl.when((shift == 0) | (mate == 0))
        def _():
            pl.semaphore_wait(barrier, 1)

        pl.semaphore_signal(far_sem, inc=1, device_id=(sibling, z), device_id_type=MESH)

    @pl.when(c == 0)
    def _():
        pl.semaphore_wait(far_sem, 1)

    wait_bytes(land.at[pl.ds(0, (N - 1) * rows), :], recv_sem.at[0])
    acc = land[pl.ds(0, rows), :].astype(jnp.float32)
    for k in range(1, N):
        acc = acc + land[pl.ds(k * rows, rows), :].astype(jnp.float32)
    slab = acc.astype(jnp.bfloat16)
    came = slab_of(down)

    @pl.when(shift == 0)
    def _():
        gfull[came, :] = slab

    @pl.when(shift != 0)
    def _():
        summed[...] = slab
        remote(summed, gfull.at[slab_of(z), :], 1, r, up).start()

    loads[2].wait()
    for peer in peers:
        remote(lfull.at[own, :], lfull.at[own, :], 2, peer, z).start()
    loads[3].wait()
    loads[4].wait()
    holder = rep_of((z + NZ - r) % NZ)

    @pl.when(holder == r)
    def _():
        moments_land[...] = moments_v[...]

    @pl.when(holder != r)
    def _():
        remote(moments_v, moments_land, 3, holder, z).start()
        wait_bytes(moments_v, recv_sem.at[3])

    @pl.when(shift != 0)
    def _():
        wait_bytes(summed, recv_sem.at[1])

    piece = gfull.at[came, :]
    def send_slab(reps):
        for peer in reps:
            pltpu.make_async_remote_copy(
                src_ref=piece,
                dst_ref=piece,
                send_sem=send_sem.at[4],
                recv_sem=slab_sem.at[k_own],
                device_id=(peer, z),
                device_id_type=MESH,
            ).start()

    def hand_over(piece, k):
        pltpu.make_async_remote_copy(
            src_ref=piece,
            dst_ref=piece,
            send_sem=send_sem.at[6],
            recv_sem=hand_sem.at[k],
            device_id=(sibling, z),
            device_id_type=MESH,
        ).start()

    def blend(moments, grad):
        one = 0.9 * moments[0] + 0.1 * grad
        two = 0.95 * moments[1] + 0.05 * grad * grad
        return one, two

    def fold(v):
        v = v * v
        v = sum(v[:, 128 * k : 128 * (k + 1)] for k in range(v.shape[1] // 128))
        return jnp.sum(v, axis=0, keepdims=True)

    send_slab(same[:5])
    hand_over(piece, k_own)
    one, two = blend(moments_land[...], gfull[came, :].astype(jnp.float32))
    adam_part = fold(one / (jnp.sqrt(two) + 1e-08))
    sums_v[...] = adam_part
    sums_land[r] = adam_part
    for peer in peers:
        remote(sums_v, sums_land.at[r], 5, peer, z).start()
    send_slab(same[5:])

    for load in loads[5:]:
        load.wait()
    wait_bytes(lfull.at[pl.ds(0, (N - 1) * rows), :], recv_sem.at[2])

    def wait_slabs(late):
        for k in reversed(range(HALF)):
            plane = first_hand[k]

            @pl.when(((lax.div(plane, 8) == 2) == late) & (k_own != k))
            def _():
                piece = gfull.at[slab_of(plane), :]
                wait_bytes(piece, slab_sem.at[k])
                hand_over(piece, k)

        for k in reversed(range(HALF)):
            plane = second_hand[k]

            @pl.when((lax.div(plane, 8) == 2) == late)
            def _():
                wait_bytes(gfull.at[slab_of(plane), :], hand_sem.at[k])

    wide = 128
    first = r * rows
    window = pl.ds(pl.multiple_of((first // wide) * wide, wide), wide)
    at = lax.broadcasted_iota(jnp.int32, (rows, wide), 1)
    want = lax.broadcasted_iota(jnp.int32, (rows, wide), 0) + first % wide
    pick = jnp.where(at == want, 1.0, 0.0).astype(jnp.bfloat16)

    def half_part(ks):
        return jnp.dot(lfull[:, ks], gfull[ks, :], preferred_element_type=jnp.float32)

    def right_part(ks):
        cols = lax.dot_general(pick, gfull[ks, window], NT, preferred_element_type=jnp.float32)
        return jnp.dot(cols.astype(jnp.bfloat16), gfull[ks, :], preferred_element_type=jnp.float32)

    early = (pl.ds(0, 256), pl.ds(384, 128))
    late = pl.ds(256, 128)
    wait_slabs(False)
    pre_v[...] = half_part(early[0]) + half_part(early[1])
    right_gram = right_part(early[0]) + right_part(early[1])
    wait_bytes(land.at[pl.ds(0, (N - 1) * rows), :], send_sem.at[0])

    @pl.when(shift != 0)
    def _():
        wait_bytes(summed, send_sem.at[1])

    wait_bytes(lfull.at[pl.ds(0, (N - 1) * rows), :], send_sem.at[2])

    @pl.when(holder != r)
    def _():
        wait_bytes(moments_v, send_sem.at[3])

    wait_slabs(True)
    half_v[...] = (pre_v[...] + half_part(late)).astype(jnp.bfloat16)
    pre_part = jnp.zeros((1, 128), jnp.float32)
    for k in range(total_rows // chunk):
        part = pl.ds(k * chunk, chunk)
        precond = jnp.dot(half_v[part, :], rroot_v[...], preferred_element_type=jnp.float32)
        pre_v[part, :] = precond
        pre_part = pre_part + fold(precond)
    gram = lax.dot_general(gfull[own, :], gfull[...], NT, preferred_element_type=jnp.float32)
    left_ref[...] = 0.9 * sleft_v[...] + 0.1 * gram
    right_ref[...] = 0.9 * sright_v[...] + 0.1 * (right_gram + right_part(late))
    one, two = blend(moments_v[...], gfull[own, :].astype(jnp.float32))
    one_ref[...] = one
    two_ref[...] = two
    pre_sum = jnp.sum(pre_part, axis=1, keepdims=True)

    wait_bytes(sums_land.at[pl.ds(0, N - 1)], recv_sem.at[5])
    adam_sum = jnp.sum(jnp.sum(sums_land[...], axis=0), axis=1, keepdims=True)
    update_ref[...] = jnp.sqrt(adam_sum / (pre_sum + 1e-06)) * pre_v[own, :]
    wait_bytes(gfull.at[pl.ds(0, (HALF - 1) * rows), :], send_sem.at[4])
    wait_bytes(gfull.at[pl.ds(0, HALF * rows), :], send_sem.at[6])
    wait_bytes(sums_land.at[pl.ds(0, N - 1)], send_sem.at[5])


def store_kernel(*refs):
    half = len(refs) // 2
    for src, dst in zip(refs[:half], refs[half:]):
        dst[...] = src[...]


def on_device(
    grad_partial,
    owner_slot,
    left_root,
    right_root,
    stat_left,
    stat_right,
    first_moment,
    second_moment,
):
    _, rows, nb, b = grad_partial.shape
    f32, bf16 = jnp.float32, jnp.bfloat16
    hbm = pl.BlockSpec(memory_space=pltpu.HBM)
    vmem = pl.BlockSpec(memory_space=pltpu.VMEM)
    shapes = [jax.ShapeDtypeStruct((rows, b), f32)] * 5
    outs = pl.pallas_call(
        step_kernel,
        out_shape=shapes,
        in_specs=[hbm] * 8,
        out_specs=[vmem] * 5,
        scratch_shapes=[
            pltpu.SMEM((nb,), jnp.int32),
            pltpu.VMEM((rows * nb, b), bf16),
            pltpu.VMEM((rows * nb, b), bf16),
            pltpu.VMEM((rows * N, b), bf16),
            pltpu.VMEM((rows, b), bf16),
            pltpu.VMEM((b, b), bf16),
            pltpu.VMEM((b, b), bf16),
            pltpu.VMEM((b, b), bf16),
            pltpu.VMEM((rows, b), f32),
            pltpu.VMEM((rows, b), f32),
            pltpu.VMEM((2, rows, b), f32),
            pltpu.VMEM((2, rows, b), f32),
            pltpu.VMEM((b, b), bf16),
            pltpu.VMEM((b, b), f32),
            pltpu.VMEM((1, 128), f32),
            pltpu.VMEM((N, 1, 128), f32),
            pltpu.SemaphoreType.DMA((8,)),
            pltpu.SemaphoreType.DMA((7,)),
            pltpu.SemaphoreType.DMA((6,)),
            pltpu.SemaphoreType.DMA((HALF,)),
            pltpu.SemaphoreType.DMA((HALF,)),
            pltpu.SemaphoreType.REGULAR,
            pltpu.SemaphoreType.REGULAR,
        ],
        compiler_params=pltpu.CompilerParams(
            collective_id=0, has_side_effects=True, vmem_limit_bytes=32 * 1024 * 1024
        ),
        name="shampoo_step",
    )(
        *[
            pltpu.with_memory_space_constraint(v, pltpu.HBM)
            for v in (
                owner_slot,
                grad_partial.reshape(rows * nb, b),
                left_root[0],
                right_root[0],
                stat_left[0],
                stat_right[0],
                first_moment[0],
                second_moment[0],
            )
        ]
    )
    outs = pl.pallas_call(
        store_kernel,
        out_shape=shapes,
        in_specs=[vmem] * 5,
        out_specs=[vmem] * 5,
        compiler_params=pltpu.CompilerParams(vmem_limit_bytes=4 * 1024 * 1024),
        name="store_results",
    )(*outs)
    return tuple(out[None] for out in outs)


def solution(mesh):
    in_specs = (
        P("rep", "blk", None, None),
        P(),
        P("blk", "rep", None),
        P("blk", None, None),
        P("blk", "rep", None),
        P("blk", "rep", None),
        P("blk", "rep", None),
        P("blk", "rep", None),
    )
    out_specs = (P("blk", "rep", None),) * 5
    return jax.shard_map(
        on_device, mesh=mesh, in_specs=in_specs, out_specs=out_specs, check_vma=False
    )
```

```python
import functools

import jax
import jax.numpy as jnp
from jax import lax
from jax.experimental import pallas as pl
from jax.experimental.pallas import tpu as pltpu
from jax.sharding import PartitionSpec as P

MESH = pl.DeviceIdType.MESH
NX, NY, NC, NZ = 4, 4, 2, 32
N = NX * NY * NC
NT = (((1,), (1,)), ((), ()))


HALF = N // NC


def chip_distance(step):
    return min(step[0], NX - step[0]) + min(step[1], NY - step[1])


CHIPS = [(dx, dy) for dx in range(NX) for dy in range(NY)]
PEERS = sorted(
    [(dx, dy, dc) for dx, dy in CHIPS for dc in range(NC) if dx or dy or dc],
    key=chip_distance,
    reverse=True,
)


SAME = [(dx, dy) for dx, dy, dc in PEERS if dc == 0]

FAR = (1, 5, 2, 7, 4, 0, 3, 6)
NEAR = (1, 0, 3, 2, 5, 4, 7, 6)


def entry(table, k):
    value = table[0] + 0 * k
    for i in range(1, len(table)):
        value = jnp.where(k == i, table[i], value)
    return value


def rep_of(shift):
    high = shift // 16
    rank = high * (2 * (shift - 16)) + (1 - high) * (2 * (15 - shift) + 1)
    tier, k = rank // 8, rank % 8
    near, odd = tier // 2, tier % 2
    core = 1 - near
    j = core * entry(FAR, k) + near * entry(NEAR, k)
    x = j // 2
    y = 2 * (j % 2) + (odd + x) % 2
    return (x * NY + y) * NC + core


def shift_of(rep):
    x, y, core = rep // (NY * NC), (rep // NC) % NY, rep % NC
    j = x * 2 + y // 2
    far = entry([FAR.index(i) for i in range(8)], j)
    near = entry([NEAR.index(i) for i in range(8)], j)
    rank = (2 * (1 - core) + (x + y) % 2) * 8 + core * far + (1 - core) * near
    odd = rank % 2
    return (1 - odd) * (16 + rank // 2) + odd * (15 - rank // 2)


def shift_at(k, near):
    return 16 + k // 2 + 8 * near if k % 2 == 0 else 15 - k // 2 - 8 * near


def step_kernel(
    owner_hbm,
    grad_hbm,
    lroot_hbm,
    rroot_hbm,
    sleft_hbm,
    sright_hbm,
    mone_hbm,
    mtwo_hbm,
    update_ref,
    left_ref,
    right_ref,
    one_ref,
    two_ref,
    owner_s,
    grad_v,
    ordered,
    land,
    summed,
    gfull,
    lfull,
    rroot_v,
    sleft_v,
    sright_v,
    moments_v,
    moments_land,
    half_v,
    pre_v,
    sums_v,
    sums_land,
    load_sem,
    send_sem,
    recv_sem,
    slab_sem,
    hand_sem,
    plane_sem,
    far_sem,
):
    r = lax.axis_index("rep")
    z = lax.axis_index("blk")
    rows = summed.shape[0]
    x, y, c = r // (NY * NC), (r // NC) % NY, r % NC
    shift = shift_of(r)
    up = (z + shift) % NZ
    down = (z + NZ - shift) % NZ
    sibling = r + 1 - 2 * c

    def peer_of(step):
        dx, dy, dc = step
        return (lax.rem(x + dx, NX) * NY + lax.rem(y + dy, NY)) * NC + lax.rem(c + dc, NC)

    def slab_of(index):
        return pl.ds(pl.multiple_of(index * rows, rows), rows)

    def remote(src, dst, k, rep, blk):
        return pltpu.make_async_remote_copy(
            src_ref=src,
            dst_ref=dst,
            send_sem=send_sem.at[k],
            recv_sem=recv_sem.at[k],
            device_id=(rep, blk),
            device_id_type=MESH,
        )

    def wait_bytes(ref, sem):
        pltpu.make_async_copy(ref, ref, sem).wait()

    own = slab_of(r)
    pairs = [
        (grad_hbm, grad_v),
        (owner_hbm, owner_s),
        (lroot_hbm, lfull.at[own, :]),
        (mone_hbm, moments_v.at[0]),
        (mtwo_hbm, moments_v.at[1]),
        (rroot_hbm, rroot_v),
        (sleft_hbm, sleft_v),
        (sright_hbm, sright_v),
    ]
    loads = [pltpu.make_async_copy(src, dst, load_sem.at[k]) for k, (src, dst) in enumerate(pairs)]
    loads[0].start()
    loads[1].start()

    barrier = pltpu.get_barrier_semaphore()
    for dx, dy in sorted(CHIPS, key=chip_distance, reverse=True):
        chip = peer_of((dx, dy, 0)) - c
        if dx or dy:
            pl.semaphore_signal(barrier, inc=1, device_id=(chip, z), device_id_type=MESH)

    @pl.when(c == 1)
    def _():
        pl.semaphore_signal(barrier, inc=1, device_id=(sibling, z), device_id_type=MESH)

    @pl.when(shift != 0)
    def _():
        pl.semaphore_signal(barrier, inc=1, device_id=(r - c + 1, down), device_id_type=MESH)

    for load in loads[2:]:
        load.start()

    total_rows = grad_v.shape[0]
    nb = total_rows // rows
    lane = lax.broadcasted_iota(jnp.int32, (1, total_rows), 1)
    loads[1].wait()
    target = jnp.zeros((1, total_rows), jnp.int32)
    for b in range(nb):
        target = jnp.where(lane % nb == b, owner_s[b], target)
    target = rep_of((target + (NZ - z)) % NZ) * rows + lane // nb
    loads[0].wait()
    chunk = 128
    for k in range(total_rows // chunk):
        row = lax.broadcasted_iota(jnp.int32, (chunk, total_rows), 0) + k * chunk
        pick = jnp.where(row == target, 1.0, 0.0).astype(jnp.bfloat16)
        part = jnp.dot(pick, grad_v[...], preferred_element_type=jnp.float32)
        ordered[pl.ds(k * chunk, chunk), :] = part.astype(jnp.bfloat16)

    targets = []
    for tier in range(4):
        core, odd = 1 - tier // 2, tier % 2
        for dx, m in ((2, 1), (2, 0), (1, 1), (3, 1), (0, 1), (1, 0), (3, 0), (0, 0)):
            px = lax.rem(x + dx, NX)
            py = lax.rem(y + 2 * m + lax.rem(odd + px + y, 2), NY)
            targets.append((px * NY + py) * NC + core)
    peers = [peer_of(step) for step in PEERS]
    same = [peer_of((dx, dy, 0)) for dx, dy in SAME]

    first_hand = [lax.rem(z + NZ - shift_at(k, 1 - c), NZ) for k in range(HALF)]
    second_hand = [lax.rem(z + NZ - shift_at(k, c), NZ) for k in range(HALF)]
    k_own = sum(jnp.where(down == first_hand[k], k, 0) for k in range(HALF))

    @pl.when(c == 0)
    def _():
        pl.semaphore_wait(barrier, N - 1)
        pl.semaphore_signal(plane_sem, inc=1, device_id=(sibling, z), device_id_type=MESH)

    @pl.when(c == 1)
    def _():
        pl.semaphore_wait(plane_sem, 1)

    def scatter_to(peer):
        remote(ordered.at[slab_of(peer), :], land.at[own, :], 0, peer, z).start()

    def is_above(peer):
        j = 2 * lax.div(peer, NY * NC) + lax.rem(lax.div(peer, 2 * NC), 2)
        return (j < 2) | (j > 4)

    above = [is_above(peer) for peer in targets[:8]]
    for peer, up_first in zip(targets[:8], above):
        pl.when((peer != r) & up_first)(functools.partial(scatter_to, peer))
    for peer, up_first in zip(targets[:8], above):
        pl.when((peer != r) & jnp.logical_not(up_first))(functools.partial(scatter_to, peer))
    for i, peer in enumerate(targets[8:]):
        if i % 8 < 7:
            scatter_to(peer)
        else:
            pl.when(peer != r)(functools.partial(scatter_to, peer))

    land[own, :] = ordered[own, :]

    @pl.when(c == 1)
    def _():
        mate = shift_of(sibling)

        @pl.when((shift != 0) & (mate != 0))
        def _():
            pl.semaphore_wait(barrier, 2)

        @pl.when((shift == 0) | (mate == 0))
        def _():
            pl.semaphore_wait(barrier, 1)

        pl.semaphore_signal(far_sem, inc=1, device_id=(sibling, z), device_id_type=MESH)

    @pl.when(c == 0)
    def _():
        pl.semaphore_wait(far_sem, 1)

    wait_bytes(land.at[pl.ds(0, (N - 1) * rows), :], recv_sem.at[0])
    acc = land[pl.ds(0, rows), :].astype(jnp.float32)
    for k in range(1, N):
        acc = acc + land[pl.ds(k * rows, rows), :].astype(jnp.float32)
    slab = acc.astype(jnp.bfloat16)
    came = slab_of(down)

    @pl.when(shift == 0)
    def _():
        gfull[came, :] = slab

    @pl.when(shift != 0)
    def _():
        summed[...] = slab
        remote(summed, gfull.at[slab_of(z), :], 1, r, up).start()

    loads[2].wait()
    for peer in peers:
        remote(lfull.at[own, :], lfull.at[own, :], 2, peer, z).start()
    loads[3].wait()
    loads[4].wait()
    holder = rep_of((z + NZ - r) % NZ)

    @pl.when(holder == r)
    def _():
        moments_land[...] = moments_v[...]

    @pl.when(holder != r)
    def _():
        remote(moments_v, moments_land, 3, holder, z).start()
        wait_bytes(moments_v, recv_sem.at[3])

    @pl.when(shift != 0)
    def _():
        wait_bytes(summed, recv_sem.at[1])

    piece = gfull.at[came, :]
    def send_slab(reps):
        for peer in reps:
            pltpu.make_async_remote_copy(
                src_ref=piece,
                dst_ref=piece,
                send_sem=send_sem.at[4],
                recv_sem=slab_sem.at[k_own],
                device_id=(peer, z),
                device_id_type=MESH,
            ).start()

    def hand_over(piece, k):
        pltpu.make_async_remote_copy(
            src_ref=piece,
            dst_ref=piece,
            send_sem=send_sem.at[6],
            recv_sem=hand_sem.at[k],
            device_id=(sibling, z),
            device_id_type=MESH,
        ).start()

    def blend(moments, grad):
        one = 0.9 * moments[0] + 0.1 * grad
        two = 0.95 * moments[1] + 0.05 * grad * grad
        return one, two

    def fold(v):
        v = v * v
        v = sum(v[:, 128 * k : 128 * (k + 1)] for k in range(v.shape[1] // 128))
        return jnp.sum(v, axis=0, keepdims=True)

    send_slab(same[:5])
    hand_over(piece, k_own)
    one, two = blend(moments_land[...], gfull[came, :].astype(jnp.float32))
    adam_part = fold(one / (jnp.sqrt(two) + 1e-08))
    sums_v[...] = adam_part
    sums_land[r] = adam_part
    for peer in peers:
        remote(sums_v, sums_land.at[r], 5, peer, z).start()
    send_slab(same[5:])

    for load in loads[5:]:
        load.wait()
    wait_bytes(lfull.at[pl.ds(0, (N - 1) * rows), :], recv_sem.at[2])

    def wait_slabs(late):
        for k in reversed(range(HALF)):
            plane = first_hand[k]

            @pl.when(((lax.div(plane, 8) == 2) == late) & (k_own != k))
            def _():
                piece = gfull.at[slab_of(plane), :]
                wait_bytes(piece, slab_sem.at[k])
                hand_over(piece, k)

        for k in reversed(range(HALF)):
            plane = second_hand[k]

            @pl.when((lax.div(plane, 8) == 2) == late)
            def _():
                wait_bytes(gfull.at[slab_of(plane), :], hand_sem.at[k])

    wide = 128
    first = r * rows
    window = pl.ds(pl.multiple_of((first // wide) * wide, wide), wide)
    at = lax.broadcasted_iota(jnp.int32, (rows, wide), 1)
    want = lax.broadcasted_iota(jnp.int32, (rows, wide), 0) + first % wide
    pick = jnp.where(at == want, 1.0, 0.0).astype(jnp.bfloat16)

    def half_part(ks):
        return jnp.dot(lfull[:, ks], gfull[ks, :], preferred_element_type=jnp.float32)

    def right_part(ks):
        cols = lax.dot_general(pick, gfull[ks, window], NT, preferred_element_type=jnp.float32)
        return jnp.dot(cols.astype(jnp.bfloat16), gfull[ks, :], preferred_element_type=jnp.float32)

    early = (pl.ds(0, 256), pl.ds(384, 128))
    late = pl.ds(256, 128)
    wait_slabs(False)
    pre_v[...] = half_part(early[0]) + half_part(early[1])
    right_gram = right_part(early[0]) + right_part(early[1])
    wait_bytes(land.at[pl.ds(0, (N - 1) * rows), :], send_sem.at[0])

    @pl.when(shift != 0)
    def _():
        wait_bytes(summed, send_sem.at[1])

    wait_bytes(lfull.at[pl.ds(0, (N - 1) * rows), :], send_sem.at[2])

    @pl.when(holder != r)
    def _():
        wait_bytes(moments_v, send_sem.at[3])

    wait_slabs(True)
    half_v[...] = (pre_v[...] + half_part(late)).astype(jnp.bfloat16)
    pre_part = jnp.zeros((1, 128), jnp.float32)
    for k in range(total_rows // chunk):
        part = pl.ds(k * chunk, chunk)
        precond = jnp.dot(half_v[part, :], rroot_v[...], preferred_element_type=jnp.float32)
        pre_v[part, :] = precond
        pre_part = pre_part + fold(precond)
    gram = lax.dot_general(gfull[own, :], gfull[...], NT, preferred_element_type=jnp.float32)
    left_ref[...] = 0.9 * sleft_v[...] + 0.1 * gram
    right_ref[...] = 0.9 * sright_v[...] + 0.1 * (right_gram + right_part(late))
    one, two = blend(moments_v[...], gfull[own, :].astype(jnp.float32))
    one_ref[...] = one
    two_ref[...] = two
    pre_sum = jnp.sum(pre_part, axis=1, keepdims=True)

    wait_bytes(sums_land.at[pl.ds(0, N - 1)], recv_sem.at[5])
    adam_sum = jnp.sum(jnp.sum(sums_land[...], axis=0), axis=1, keepdims=True)
    update_ref[...] = jnp.sqrt(adam_sum / (pre_sum + 1e-06)) * pre_v[own, :]
    wait_bytes(gfull.at[pl.ds(0, (HALF - 1) * rows), :], send_sem.at[4])
    wait_bytes(gfull.at[pl.ds(0, HALF * rows), :], send_sem.at[6])
    wait_bytes(sums_land.at[pl.ds(0, N - 1)], send_sem.at[5])


def store_kernel(*refs):
    half = len(refs) // 2
    for src, dst in zip(refs[:half], refs[half:]):
        dst[...] = src[...]


def on_device(
    grad_partial,
    owner_slot,
    left_root,
    right_root,
    stat_left,
    stat_right,
    first_moment,
    second_moment,
):
    _, rows, nb, b = grad_partial.shape
    f32, bf16 = jnp.float32, jnp.bfloat16
    hbm = pl.BlockSpec(memory_space=pltpu.HBM)
    vmem = pl.BlockSpec(memory_space=pltpu.VMEM)
    shapes = [jax.ShapeDtypeStruct((rows, b), f32)] * 5
    outs = pl.pallas_call(
        step_kernel,
        out_shape=shapes,
        in_specs=[hbm] * 8,
        out_specs=[vmem] * 5,
        scratch_shapes=[
            pltpu.SMEM((nb,), jnp.int32),
            pltpu.VMEM((rows * nb, b), bf16),
            pltpu.VMEM((rows * nb, b), bf16),
            pltpu.VMEM((rows * N, b), bf16),
            pltpu.VMEM((rows, b), bf16),
            pltpu.VMEM((b, b), bf16),
            pltpu.VMEM((b, b), bf16),
            pltpu.VMEM((b, b), bf16),
            pltpu.VMEM((rows, b), f32),
            pltpu.VMEM((rows, b), f32),
            pltpu.VMEM((2, rows, b), f32),
            pltpu.VMEM((2, rows, b), f32),
            pltpu.VMEM((b, b), bf16),
            pltpu.VMEM((b, b), f32),
            pltpu.VMEM((1, 128), f32),
            pltpu.VMEM((N, 1, 128), f32),
            pltpu.SemaphoreType.DMA((8,)),
            pltpu.SemaphoreType.DMA((7,)),
            pltpu.SemaphoreType.DMA((6,)),
            pltpu.SemaphoreType.DMA((HALF,)),
            pltpu.SemaphoreType.DMA((HALF,)),
            pltpu.SemaphoreType.REGULAR,
            pltpu.SemaphoreType.REGULAR,
        ],
        compiler_params=pltpu.CompilerParams(
            collective_id=0, has_side_effects=True, vmem_limit_bytes=32 * 1024 * 1024
        ),
        name="shampoo_step",
    )(
        *[
            pltpu.with_memory_space_constraint(v, pltpu.HBM)
            for v in (
                owner_slot,
                grad_partial.reshape(rows * nb, b),
                left_root[0],
                right_root[0],
                stat_left[0],
                stat_right[0],
                first_moment[0],
                second_moment[0],
            )
        ]
    )
    outs = pl.pallas_call(
        store_kernel,
        out_shape=shapes,
        in_specs=[vmem] * 5,
        out_specs=[vmem] * 5,
        compiler_params=pltpu.CompilerParams(vmem_limit_bytes=4 * 1024 * 1024),
        name="store_results",
    )(*outs)
    return tuple(out[None] for out in outs)


def solution(mesh):
    in_specs = (
        P("rep", "blk", None, None),
        P(),
        P("blk", "rep", None),
        P("blk", None, None),
        P("blk", "rep", None),
        P("blk", "rep", None),
        P("blk", "rep", None),
        P("blk", "rep", None),
    )
    out_specs = (P("blk", "rep", None),) * 5
    return jax.shard_map(
        on_device, mesh=mesh, in_specs=in_specs, out_specs=out_specs, check_vma=False
    )
```
